128 devices in a mesh: expert: 16 (over x, y), etp: 2 (over core), dp: 4 (over z).
Axes of the slice: x: 4, y: 4, z: 4, core: 2. Of those that a mesh axis runs over, the one named last changes fastest.
Arguments:
- frames: bfloat16 [24576, 1024], P(('expert', 'dp'), 'etp'), may hold values from -6 to 6
- out_grad: bfloat16 [24576, 1024], P(('expert', 'dp'), 'etp'), may hold values from -6 to 6
- routes: int32 [24576, 2], P(('expert', 'dp')), may hold values from 0 to 31, all different within a row; in each aligned block of 384 rows (0 to 383, 384 to 767, ...) at most 48 rows name the same one
- gate_levels: int32 [24576, 2], P(('expert', 'dp')), may hold values from 16 to 255
- w_gate: bfloat16 [32, 1024, 2048], P('expert', None, 'etp'), may hold values from -0.1875 to 0.1875
- w_up: bfloat16 [32, 1024, 2048], P('expert', None, 'etp'), may hold values from -0.1875 to 0.1875
- w_down: bfloat16 [32, 1024, 2048], P('expert', None, 'etp'), may hold values from -0.125 to 0.125
Outputs:
- frame_grad: bfloat16 [24576, 1024], P(('expert', 'dp'), 'etp')
- gate_wgrad: bfloat16 [32, 1024, 2048], P('expert', 'dp', 'etp')
- up_wgrad: bfloat16 [32, 1024, 2048], P('expert', 'dp', 'etp')
- down_wgrad: bfloat16 [32, 1024, 2048], P('expert', 'dp', 'etp')
The draws below stay inside these ranges and needn't reach their ends.
Inputs may be any that keep to these rules, and one draw needn't show every extreme that they name: `routes`: within the 384 frames of one device, no expert is named more than 48 times over both columns, and in every draw some expert is named exactly 48 times there; the two choices of a frame differ.
All inputs are finite; a program needn't handle non-finite values.
Results may differ from the reference program's by a relative error of at most 0.014.
Values may be sent and summed in bfloat16 or wider, within the bound.
A program may use at most 128 MiB of HBM per device.

```python
import math
import jax
import jax.numpy as jnp
import numpy as np
from jax import lax

D = 1024
FF = 2048
TOK_DEV = 384
EXPERTS = 32
CAP = 48
TOKENS = 24576
N_EXPERT = 16
N_DP = 4


def touch_ends(result, rng, least, high):
    shape = result.shape
    place = [jax.random.randint(jax.random.fold_in(rng, axis), (), 0, shape[axis]) for axis in range(len(shape))]
    result = result.at[tuple(place)].set(least)
    longest = shape.index(max(shape))
    place[longest] = (place[longest] + 1) % shape[longest]
    return result.at[tuple(place)].set(high)


def level_of(own_key, shape, shards, low, largest):
    level = 1.0
    for dim, blocks in shards:
        draws = jax.random.uniform(jax.random.fold_in(jax.random.fold_in(own_key, 6), dim), (blocks,), jnp.float32, low / len(shards), largest / len(shards))
        level = level * jnp.repeat(jnp.exp(draws), shape[dim] // blocks).reshape((-1,) + (1,) * (len(shape) - 1 - dim))
    return level


def shared_out(stream_key, own, number, rows, number_of, top, reach, lean):
    ranking = jax.random.permutation(stream_key, number_of)
    packed, ordinary = shares(number_of, rows * top, reach, lean, True), shares(number_of, rows * top, reach, lean, False)
    places = jnp.arange(number_of)

    def named(sizes, rotation):
        used = int((sizes > 0).sum())
        fixed = max(1, used // 4)
        moved = fixed + (places - fixed + rotation * (used - fixed)) % max(1, number_of - fixed)
        return jnp.zeros((number_of,), jnp.int32).at[ranking[jnp.where(places < fixed, places, moved)]].set(jnp.asarray(sizes, jnp.int32))

    sizes = jnp.where(number % 4 == 0, named(packed, number // 4), named(ordinary, number - number // 4 - 1))
    mixed = jax.random.permutation(jax.random.fold_in(own, 3), number_of)
    donor, receiver = mixed[0:number_of // 2 * 2:2], mixed[1:number_of // 2 * 2:2]
    slack = jnp.minimum(sizes[donor] - 1, reach - sizes[receiver]) // 2
    slack = jnp.where((donor == ranking[0]) | (receiver == ranking[0]) | (sizes[receiver] == 0), 0, jnp.maximum(slack, 0))
    moved = jax.random.randint(jax.random.fold_in(own, 4), (number_of // 2,), 0, 1 << 20) % (slack + 1)
    sizes = sizes.at[donor].add(-moved).at[receiver].add(moved)
    items = jnp.searchsorted(jnp.cumsum(sizes), jnp.arange(rows * top), side="right").astype(jnp.int32)
    listing = items.reshape(top, rows).T
    listing = listing[jax.random.permutation(jax.random.fold_in(own, 1), rows)]
    rotation = jax.random.randint(jax.random.fold_in(own, 2), (rows, 1), 0, top)
    return jnp.take_along_axis(listing, (jnp.arange(top)[None, :] + rotation) % top, axis=1)


def shares(number_of, total, reach, skew, full):
    portions = [(1 << 20) // math.isqrt(grade ** skew) + 1 for grade in range(1, number_of + 1)]
    largest = reach if full else min(reach, max(-(-total // number_of), total * portions[0] // sum(portions)))
    least = 1 if total - largest >= number_of - 1 else 0
    holding, surplus = [largest] + [least] * (number_of - 1), total - largest - least * (number_of - 1)
    while surplus > 0:
        movable = [i for i in range(1, number_of) if holding[i] < largest] or [i for i in range(1, number_of) if holding[i] < reach]
        mass, left = sum([portions[i] for i in movable]), surplus
        for i in movable:
            extra = min(reach - holding[i], max(1, left * portions[i] // mass), surplus)
            holding[i] = holding[i] + extra
            surplus = surplus - extra
    return np.array(holding)


def gaussian(rng, shape, width, reach, shards=(), kind=jnp.bfloat16):
    entries = width * jax.random.normal(rng, shape, jnp.float32)
    if shards:
        entries = entries * level_of(rng, shape, shards, -0.22, 0.18)
    return jnp.clip(entries, -reach, reach).astype(kind)


def setup_inputs(seed: int = 0) -> dict:
    streams_of = jax.random.split(jax.random.key(seed), 8)
    frames = gaussian(streams_of[0], (TOKENS, D), 1.0, 6.0, ((0, 64), (1, 2)))
    out_grad = gaussian(streams_of[1], (TOKENS, D), 1.0, 6.0, ((0, 64), (1, 2)))
    routes_keys = jax.random.split(jax.random.fold_in(streams_of[2], 1), TOKENS // TOK_DEV)
    routes_turns = jax.random.permutation(jax.random.fold_in(streams_of[2], 3), TOKENS // TOK_DEV)
    routes = jax.vmap(lambda own, number: shared_out(jax.random.fold_in(streams_of[2], 2), own, number, TOK_DEV, EXPERTS, 2, CAP, 1))(routes_keys, routes_turns).reshape((TOKENS, 2))
    gate_levels = touch_ends(jax.random.randint(streams_of[3], (TOKENS, 2), 16, 256), jax.random.fold_in(streams_of[3], 1), 16, 255).astype(jnp.int32)
    w_gate = gaussian(streams_of[4], (EXPERTS, D, FF), D ** -0.5, 0.1875, ((0, 16), (2, 2)))
    w_up = gaussian(streams_of[5], (EXPERTS, D, FF), D ** -0.5, 0.1875, ((0, 16), (2, 2)))
    w_down = gaussian(streams_of[6], (EXPERTS, D, FF), FF ** -0.5, 0.125, ((0, 16), (2, 2)))
    return dict(frames=frames, out_grad=out_grad, routes=routes, gate_levels=gate_levels, w_gate=w_gate, w_up=w_up, w_down=w_down)


def expert_grads(rows_in, rows_grad, gate_mat, up_mat, down_mat):
    pre_gate = jnp.dot(rows_in, gate_mat, preferred_element_type=jnp.float32)
    pre_up = jnp.dot(rows_in, up_mat, preferred_element_type=jnp.float32)
    sigmoid_gate = jax.nn.sigmoid(pre_gate)
    activated = pre_gate * sigmoid_gate
    hidden = (activated * pre_up).astype(jnp.bfloat16)
    hidden_grad = jnp.dot(rows_grad, down_mat, preferred_element_type=jnp.float32)
    gate_in = (hidden_grad * pre_up * sigmoid_gate * (1.0 + pre_gate * (1.0 - sigmoid_gate))).astype(jnp.bfloat16)
    up_in = (hidden_grad * activated).astype(jnp.bfloat16)
    grad_gate = jnp.dot(rows_in.T, gate_in, preferred_element_type=jnp.float32)
    grad_up = jnp.dot(rows_in.T, up_in, preferred_element_type=jnp.float32)
    grad_down = jnp.dot(rows_grad.T, hidden, preferred_element_type=jnp.float32)
    input_term = jnp.dot(gate_in, gate_mat.T, preferred_element_type=jnp.float32) + jnp.dot(up_in, up_mat.T, preferred_element_type=jnp.float32)
    return grad_gate, grad_up, grad_down, input_term


def reference(frames, out_grad, routes, gate_levels, w_gate, w_up, w_down):
    tokens = frames.shape[0]
    per_item = N_EXPERT * CAP
    flat_expert = routes.reshape(-1).astype(jnp.int32)
    pair_row = (jnp.arange(2 * tokens, dtype=jnp.int32) // 2).astype(jnp.int32)
    group_of = (pair_row // TOK_DEV) % N_DP
    gate_value = gate_levels.reshape(-1).astype(jnp.float32) / 256.0

    def one_expert(expert_id):
        gate_mat = w_gate[expert_id]
        up_mat = w_up[expert_id]
        down_mat = w_down[expert_id]
        sum_gate = jnp.zeros(gate_mat.shape, jnp.float32)
        sum_up = jnp.zeros(gate_mat.shape, jnp.float32)
        sum_down = jnp.zeros(gate_mat.shape, jnp.float32)
        values = []
        places = []
        for group_id in range(N_DP):
            marked = (flat_expert == expert_id) & (group_of == group_id)
            order = jnp.argsort(jnp.where(marked, 0, 1).astype(jnp.int32), stable=True)[:per_item].astype(jnp.int32)
            valid = marked[order]
            rows = pair_row[order]
            rows_in = jnp.where(valid[:, None], frames[rows], jnp.zeros((), jnp.bfloat16))
            scaled = gate_value[order][:, None] * out_grad[rows].astype(jnp.float32)
            rows_grad = jnp.where(valid[:, None], scaled, 0.0).astype(jnp.bfloat16)
            grad_gate, grad_up, grad_down, input_term = expert_grads(rows_in, rows_grad, gate_mat, up_mat, down_mat)
            sum_gate = sum_gate + grad_gate.astype(jnp.bfloat16).astype(jnp.float32)
            sum_up = sum_up + grad_up.astype(jnp.bfloat16).astype(jnp.float32)
            sum_down = sum_down + grad_down.astype(jnp.bfloat16).astype(jnp.float32)
            values.append(jnp.where(valid[:, None], input_term, 0.0).astype(jnp.bfloat16))
            places.append(rows)
        return (sum_gate.astype(jnp.bfloat16), sum_up.astype(jnp.bfloat16), sum_down.astype(jnp.bfloat16), jnp.stack(values), jnp.stack(places))

    gate_wgrad, up_wgrad, down_wgrad, values, places = lax.map(one_expert, jnp.arange(w_gate.shape[0], dtype=jnp.int32))
    total = jnp.zeros(frames.shape, jnp.float32)
    total = total.at[places.reshape(-1)].add(values.reshape(-1, frames.shape[1]).astype(jnp.float32))
    return total.astype(jnp.bfloat16), gate_wgrad, up_wgrad, down_wgrad
```

```python
import jax
import jax.numpy as jnp
from jax import lax
from jax.experimental import pallas as pl
from jax.experimental.pallas import tpu as pltpu
from jax.sharding import PartitionSpec as P

MESH = pl.DeviceIdType.MESH
BF, F32 = jnp.bfloat16, jnp.float32
PEERS, DP = 16, 4
EXPERTS = 32
CAP = 48
TOK = 384
D = 1024
HALF = 512
FF = 1024
ROWS = 2 * PEERS * CAP
CH = 256
NCH = FF // CH
SL = D // DP
RB = 384
ANY = pl.BlockSpec(memory_space=pl.ANY)
VM = pl.BlockSpec(memory_space=pltpu.VMEM)
ORDER = (
    (1, 0), (0, 2), (3, 1), (2, 3), (0, 1), (2, 0), (1, 3), (3, 2),
    (0, 3), (1, 1), (2, 2), (3, 0), (1, 2), (2, 1), (3, 3),
)


def pack_kernel(routes_ref, levels_ref, frames_ref, grads_ref, out_ref):
    ids = lax.broadcasted_iota(jnp.int32, (EXPERTS, TOK), 0)
    first = ids == routes_ref[0:1, :]
    second = ids == routes_ref[1:2, :]
    named = first | second
    before = lax.broadcasted_iota(jnp.int32, (TOK, TOK), 0) < lax.broadcasted_iota(
        jnp.int32, (TOK, TOK), 1
    )
    count = jnp.dot(
        named.astype(F32).astype(BF), before.astype(F32).astype(BF), preferred_element_type=F32
    ).astype(jnp.int32)
    place = jnp.where(named, count, -1)
    level = jnp.where(first, levels_ref[0:1, :], levels_ref[1:2, :])
    gate = level.astype(F32) / 256.0
    step = 8
    for group in range(EXPERTS // step):
        here = place[group * step : (group + 1) * step]
        slots = lax.broadcasted_iota(jnp.int32, (step, CAP, TOK), 1)
        hit = here[:, None, :] == slots
        pick = jnp.where(hit, 1.0, 0.0).reshape(step * CAP, TOK).astype(BF)
        scaled = (
            jnp.where(hit, gate[group * step : (group + 1) * step][:, None, :], 0.0)
            .reshape(step * CAP, TOK)
            .astype(BF)
        )
        rows = pl.ds(group * step * CAP, step * CAP)
        out_ref[rows, 0:HALF] = jnp.dot(
            pick, frames_ref[...], preferred_element_type=F32
        ).astype(BF)
        out_ref[rows, HALF : 2 * HALF] = jnp.dot(
            scaled, grads_ref[...], preferred_element_type=F32
        ).astype(BF)


def unpack_kernel(routes_ref, back_ref, out_ref):
    ids = lax.broadcasted_iota(jnp.int32, (TOK, EXPERTS), 1)
    first = ids == routes_ref[:, 0:1]
    second = ids == routes_ref[:, 1:2]
    named = (first | second).astype(F32).astype(BF)
    before = lax.broadcasted_iota(jnp.int32, (TOK, TOK), 1) < lax.broadcasted_iota(
        jnp.int32, (TOK, TOK), 0
    )
    count = jnp.dot(before.astype(F32).astype(BF), named, preferred_element_type=F32)
    slot = count + (ids * CAP).astype(F32)
    slot0 = jnp.sum(jnp.where(first, slot, 0.0), axis=1, keepdims=True).astype(jnp.int32)
    slot1 = jnp.sum(jnp.where(second, slot, 0.0), axis=1, keepdims=True).astype(jnp.int32)
    lanes = lax.broadcasted_iota(jnp.int32, (TOK, EXPERTS * CAP), 1)
    pick = jnp.where((lanes == slot0) | (lanes == slot1), 1.0, 0.0).astype(BF)
    out_ref[...] = jnp.dot(pick, back_ref[...], preferred_element_type=F32).astype(BF)


def layer_kernel(
    send_ref, wg_hbm, wu_hbm, wd_hbm,
    og_ref, ou_ref, od_ref, back_ref,
    recv, wts, turned, acts, sendp, recvp, kept, own_half, sib_send, sib_recv, ret, outs, outq,
    w_sem, loc_sem, d_send, d_recv, s_send, s_recv, p_send, p_recv,
    h_send, h_recv, r_send, r_recv, rl_sem, q_send, q_recv, o_sem,
):
    e = lax.axis_index("expert")
    c = lax.axis_index("etp")
    z = lax.axis_index("dp")
    ex, ey = e // 4, lax.rem(e, 4)
    p = z + 1 - 2 * lax.rem(z, 2)
    q = 3 - z
    o = 3 - p
    own = z // 2
    out_refs = (og_ref, ou_ref, od_ref)

    wcopy = [
        pltpu.make_async_copy(w.at[own], wts.at[i], w_sem.at[i])
        for i, w in enumerate((wg_hbm, wu_hbm, wd_hbm))
    ]
    for w in wcopy:
        w.start()

    def at(dx, dy):
        ax = jnp.where(c == 1, dy, dx)
        ay = jnp.where(c == 1, dx, dy)
        return lax.rem(ex + ax, 4) * 4 + lax.rem(ey + ay, 4)

    barrier = pltpu.get_barrier_semaphore()

    def greet(i, _):
        d = lax.rem(e + i, PEERS)
        pl.semaphore_signal(barrier, inc=1, device_id=(d, c, q), device_id_type=MESH)

        @pl.when(i > 0)
        def _():
            pl.semaphore_signal(barrier, inc=1, device_id=(d, c, z), device_id_type=MESH)

        return 0

    lax.fori_loop(0, PEERS, greet, 0)
    pl.semaphore_signal(barrier, inc=1, device_id=(e, c, p), device_id_type=MESH)
    pl.semaphore_signal(barrier, inc=1, device_id=(e, 1 - c, z), device_id_type=MESH)
    pl.semaphore_wait(barrier, 2 * PEERS + 1)

    plane = (z, q)

    def rows_of(k, s):
        return pl.ds(pl.multiple_of((k * PEERS + s) * CAP, CAP), CAP)

    def give(d, k):
        return pltpu.make_async_remote_copy(
            src_ref=send_ref.at[d, own if k == 0 else 1 - own],
            dst_ref=recv.at[c, rows_of(k, e)],
            send_sem=d_send.at[k, d],
            recv_sem=d_recv.at[k, e],
            device_id=(d, c, plane[k]),
            device_id_type=MESH,
        )

    def take(s, k):
        return pltpu.make_async_remote_copy(
            src_ref=recv.at[c, rows_of(k, s)],
            dst_ref=recv.at[c, rows_of(k, s)],
            send_sem=d_send.at[k, s],
            recv_sem=d_recv.at[k, s],
            device_id=(s, c, plane[k]),
            device_id_type=MESH,
        )

    def share(half, s, k):
        return pltpu.make_async_remote_copy(
            src_ref=recv.at[half, rows_of(k, s)],
            dst_ref=recv.at[half, rows_of(k, s)],
            send_sem=s_send.at[k, s],
            recv_sem=s_recv.at[k, s],
            device_id=(e, 1 - c, z),
            device_id_type=MESH,
        )

    local = pltpu.make_async_copy(send_ref.at[e, own], recv.at[c, rows_of(0, e)], loc_sem)
    local.start()
    for k in range(2):
        for off in ORDER:
            give(at(*off), k).start()
        if k == 1:
            give(e, 1).start()
    for w in wcopy:
        w.wait()
    local.wait()
    share(c, e, 0).start()

    def arrive(k):
        for dx, dy in ORDER:
            s = at((4 - dx) % 4, (4 - dy) % 4)
            take(s, k).wait_recv()
            share(c, s, k).start()
        if k == 1:
            take(e, 1).wait_recv()
            share(c, e, 1).start()

        def mate(s, _):
            share(1 - c, s, k).wait_recv()
            return 0

        lax.fori_loop(0, PEERS, mate, 0)

    def forward(k, j, ch):
        rows = pl.ds(pl.multiple_of(k * (ROWS // 2) + j * RB, RB), RB)
        cols = pl.ds(pl.multiple_of(ch * CH, CH), CH)

        def product(i, base):
            total = jnp.dot(
                recv[0, rows, base : base + HALF], wts[i, 0:HALF, cols], preferred_element_type=F32
            )
            return total + jnp.dot(
                recv[1, rows, base : base + HALF], wts[i, HALF:D, cols], preferred_element_type=F32
            )

        pre_gate = product(0, 0)
        pre_up = product(1, 0)
        sig = jax.nn.sigmoid(pre_gate)
        act = pre_gate * sig
        acts[2, ch, rows, :] = (act * pre_up).astype(BF)
        grad = product(2, HALF)
        acts[0, ch, rows, :] = (
            grad * pre_up * sig * (1.0 + pre_gate * (1.0 - sig))
        ).astype(BF)
        acts[1, ch, rows, :] = (grad * act).astype(BF)

    def turn(k):
        def body(i, _):
            half, j = i // 2, lax.rem(i, 2)
            rows = pl.ds(pl.multiple_of(k * (ROWS // 2) + j * RB, RB), RB)
            for t in range(2):
                for h in range(2):
                    base = t * HALF + h * SL
                    block = recv[half, rows, base : base + SL]
                    turned[t, 2 * half + h, :, rows] = block.T
            return 0

        lax.fori_loop(0, 4, body, 0)

    arrive(0)
    turn(0)

    def early(i, _):
        forward(0, lax.rem(i, 2), i // 2)
        return 0

    lax.fori_loop(0, 2 * NCH, early, 0)
    arrive(1)
    turn(1)

    def to_mate(ch, m):
        return pltpu.make_async_remote_copy(
            src_ref=sendp.at[ch, m],
            dst_ref=recvp.at[ch, m],
            send_sem=p_send.at[ch, m],
            recv_sem=p_recv.at[ch, m],
            device_id=(e, c, p),
            device_id_type=MESH,
        )

    def weight_grad(m, ch, part):
        lhs = turned[0 if m < 2 else 1, part]
        return jnp.dot(lhs, acts[m, ch], preferred_element_type=F32)

    def late(ch, _):
        for j in range(2):
            forward(1, j, ch)
        for m in range(3):
            sendp[ch, m, 0] = weight_grad(m, ch, p).astype(BF)
            sendp[ch, m, 1] = weight_grad(m, ch, o).astype(BF)
            to_mate(ch, m).start()
        return 0

    lax.fori_loop(0, NCH, late, 0)

    def swap(b):
        return pltpu.make_async_remote_copy(
            src_ref=sib_send.at[b],
            dst_ref=sib_recv.at[b],
            send_sem=h_send.at[b],
            recv_sem=h_recv.at[b],
            device_id=(e, 1 - c, z),
            device_id_type=MESH,
        )

    def input_grad(i, _):
        b = lax.rem(i + 2, 4)
        rows = pl.ds(pl.multiple_of(b * RB, RB), RB)

        def half_of(h):
            feats = pl.ds(pl.multiple_of(h * HALF, HALF), HALF)
            total = jnp.zeros((RB, HALF), F32)
            for w in range(2):
                for ch in range(NCH):
                    total += lax.dot_general(
                        acts[w, ch, rows, :],
                        wts[w, feats, ch * CH : (ch + 1) * CH],
                        (((1,), (1,)), ((), ())),
                        preferred_element_type=F32,
                    )
            return total

        sib_send[b] = half_of(1 - c).astype(BF)
        swap(b).start()
        own_half[b] = half_of(c)
        return 0

    lax.fori_loop(0, 4, input_grad, 0)

    def keep(ch, _):
        for m in range(3):
            kept[ch, m, 0] = weight_grad(m, ch, z)
            kept[ch, m, 1] = weight_grad(m, ch, q)
        return 0

    lax.fori_loop(0, NCH, keep, 0)

    def give_back(s, k):
        return pltpu.make_async_remote_copy(
            src_ref=ret.at[rows_of(k, s)],
            dst_ref=back_ref.at[e, own],
            send_sem=r_send.at[k, s],
            recv_sem=r_recv.at[k, e],
            device_id=(s, c, plane[k]),
            device_id_type=MESH,
        )

    def take_back(s, k):
        return pltpu.make_async_remote_copy(
            src_ref=ret.at[rows_of(k, s)],
            dst_ref=back_ref.at[s, own if k == 0 else 1 - own],
            send_sem=r_send.at[k, s],
            recv_sem=r_recv.at[k, s],
            device_id=(s, c, plane[k]),
            device_id_type=MESH,
        )

    back_local = pltpu.make_async_copy(ret.at[rows_of(0, e)], back_ref.at[e, own], rl_sem)
    for b in (2, 3, 0, 1):
        swap(b).wait_recv()
        ret[pl.ds(b * RB, RB), :] = (own_half[b] + sib_recv[b].astype(F32)).astype(BF)
        if b == 3:
            for off in ORDER:
                give_back(at(*off), 1).start()
            give_back(e, 1).start()
        if b == 1:
            for off in ORDER:
                give_back(at(*off), 0).start()
            back_local.start()

    def to_q(ch, m):
        place = out_refs[m].at[own, :, pl.ds(pl.multiple_of(ch * CH, CH), CH)]
        return pltpu.make_async_remote_copy(
            src_ref=outq.at[ch, m],
            dst_ref=place,
            send_sem=q_send.at[ch, m],
            recv_sem=q_recv.at[ch, m],
            device_id=(e, c, q),
            device_id_type=MESH,
        )

    def from_q(ch, m):
        place = out_refs[m].at[1 - own, :, pl.ds(pl.multiple_of(ch * CH, CH), CH)]
        return pltpu.make_async_remote_copy(
            src_ref=outq.at[ch, m],
            dst_ref=place,
            send_sem=q_send.at[ch, m],
            recv_sem=q_recv.at[ch, m],
            device_id=(e, c, q),
            device_id_type=MESH,
        )

    def to_out(ch, m):
        place = out_refs[m].at[own, :, pl.ds(pl.multiple_of(ch * CH, CH), CH)]
        return pltpu.make_async_copy(outs.at[ch, m], place, o_sem.at[ch, m])

    def finish(ch, _):
        for m in range(3):
            to_mate(ch, m).wait_recv()
            outq[ch, m] = (kept[ch, m, 1] + recvp[ch, m, 1].astype(F32)).astype(BF)
            to_q(ch, m).start()
            outs[ch, m] = (kept[ch, m, 0] + recvp[ch, m, 0].astype(F32)).astype(BF)
            to_out(ch, m).start()
        return 0

    lax.fori_loop(0, NCH, finish, 0)

    def drain_peers(i, _):
        d = lax.rem(e + i, PEERS)
        give(d, 1).wait_send()
        share(c, d, 0).wait_send()
        share(c, d, 1).wait_send()
        give_back(d, 1).wait_send()
        take_back(d, 1).wait_recv()

        @pl.when(i > 0)
        def _():
            give(d, 0).wait_send()
            give_back(d, 0).wait_send()
            take_back(d, 0).wait_recv()

        return 0

    lax.fori_loop(0, PEERS, drain_peers, 0)
    back_local.wait()

    def drain(ch, _):
        swap(ch).wait_send()
        for m in range(3):
            to_mate(ch, m).wait_send()
            to_q(ch, m).wait_send()
            from_q(ch, m).wait_recv()
            to_out(ch, m).wait()
        return 0

    lax.fori_loop(0, NCH, drain, 0)


def layer(send, w_gate, w_up, w_down):
    dma = pltpu.SemaphoreType.DMA
    grad = jax.ShapeDtypeStruct((2, SL, FF), BF)
    return pl.pallas_call(
        layer_kernel,
        out_shape=[grad, grad, grad, jax.ShapeDtypeStruct((PEERS, 2, CAP, HALF), BF)],
        in_specs=[ANY] * 4,
        out_specs=[ANY] * 4,
        scratch_shapes=[
            pltpu.VMEM((2, ROWS, 2 * HALF), BF),
            pltpu.VMEM((3, D, FF), BF),
            pltpu.VMEM((2, DP, SL, ROWS), BF),
            pltpu.VMEM((3, NCH, ROWS, CH), BF),
            pltpu.VMEM((NCH, 3, 2, SL, CH), BF),
            pltpu.VMEM((NCH, 3, 2, SL, CH), BF),
            pltpu.VMEM((NCH, 3, 2, SL, CH), F32),
            pltpu.VMEM((4, RB, HALF), F32),
            pltpu.VMEM((4, RB, HALF), BF),
            pltpu.VMEM((4, RB, HALF), BF),
            pltpu.VMEM((ROWS, HALF), BF),
            pltpu.VMEM((NCH, 3, SL, CH), BF),
            pltpu.VMEM((NCH, 3, SL, CH), BF),
            dma((3,)),
            dma,
            dma((2, PEERS)),
            dma((2, PEERS)),
            dma((2, PEERS)),
            dma((2, PEERS)),
            dma((NCH, 3)),
            dma((NCH, 3)),
            dma((4,)),
            dma((4,)),
            dma((2, PEERS)),
            dma((2, PEERS)),
            dma,
            dma((NCH, 3)),
            dma((NCH, 3)),
            dma((NCH, 3)),
        ],
        compiler_params=pltpu.CompilerParams(
            collective_id=1, has_side_effects=True, vmem_limit_bytes=60 * 1024 * 1024
        ),
        cost_estimate=pl.CostEstimate(
            flops=16 * ROWS * D * FF, bytes_accessed=20_000_000, transcendentals=ROWS * FF
        ),
        name="layer",
    )(send, w_gate, w_up, w_down)


def local(frames, out_grad, routes, gate_levels, w_gate, w_up, w_down):
    send = pl.pallas_call(
        pack_kernel,
        out_shape=jax.ShapeDtypeStruct((EXPERTS * CAP, 2 * HALF), BF),
        in_specs=[VM] * 4,
        out_specs=VM,
        name="pack",
    )(routes.T, gate_levels.T, frames, out_grad)
    send = send.reshape(PEERS, 2, CAP, 2 * HALF)
    gate_grad, up_grad, down_grad, back = layer(send, w_gate, w_up, w_down)
    frame_grad = pl.pallas_call(
        unpack_kernel,
        out_shape=jax.ShapeDtypeStruct((TOK, HALF), BF),
        in_specs=[VM] * 2,
        out_specs=VM,
        name="unpack",
    )(routes, back.reshape(EXPERTS * CAP, HALF))
    return frame_grad, gate_grad, up_grad, down_grad


def solution(mesh):
    placed = (
        P(("expert", "dp"), "etp"),
        P(("expert", "dp"), "etp"),
        P(("expert", "dp"), None),
        P(("expert", "dp"), None),
        P("expert", None, "etp"),
        P("expert", None, "etp"),
        P("expert", None, "etp"),
    )
    return jax.shard_map(
        local,
        mesh=mesh,
        in_specs=placed,
        out_specs=(
            P(("expert", "dp"), "etp"),
            P("expert", "dp", "etp"),
            P("expert", "dp", "etp"),
            P("expert", "dp", "etp"),
        ),
        check_vma=False,
    )
```

```python
import jax
import jax.numpy as jnp
from jax import lax
from jax.experimental import pallas as pl
from jax.experimental.pallas import tpu as pltpu
from jax.sharding import PartitionSpec as P

MESH = pl.DeviceIdType.MESH
BF, F32 = jnp.bfloat16, jnp.float32
PEERS, DP = 16, 4
EXPERTS = 32
CAP = 48
TOK = 384
D = 1024
HALF = 512
FF = 1024
ROWS = 2 * PEERS * CAP
CH = 256
NCH = FF // CH
SL = D // DP
RB = 384
ANY = pl.BlockSpec(memory_space=pl.ANY)
VM = pl.BlockSpec(memory_space=pltpu.VMEM)


def offsets(names):
    kinds = {
        "a": [(1, 0), (3, 0)], "b": [(0, 1), (0, 3)], "c": [(1, 1), (3, 3)], "d": [(1, 3), (3, 1)],
        "e": [(2, 1), (2, 3)], "f": [(1, 2), (3, 2)], "g": [(2, 0)], "h": [(0, 2)], "i": [(2, 2)],
        "l": [(0, 0)],
    }
    return [off for name in names for off in kinds[name]]


def mirrored(off):
    return (4 - off[0]) % 4, (4 - off[1]) % 4


GROUPS = [
    (offsets(here), offsets(there))
    for here, there in zip(("lid", "af", "be", "cgh"), ("be", "dil", "cgh", "af"))
]
BLOCKS = [
    block for here, there in GROUPS for a, b in zip(here, there) for block in (a + (0,), b + (1,))
]
INDEX = {block: i for i, block in enumerate(BLOCKS)}
NBLOCK = len(BLOCKS)
SENDS = [
    BLOCKS,
    [
        block
        for here, there in GROUPS
        for a, b in zip(here, there)
        for block in (mirrored(b) + (1,), mirrored(a) + (0,))
    ],
]
GROUP = NBLOCK // 4


def layer_kernel(
    routes_ref, levels_ref, frames_ref, grads_ref, wg_hbm, wu_hbm, wd_hbm,
    og_ref, ou_ref, od_ref, frame_ref,
    place_ref, gate_ref, pick_ref, scaled_ref, send_ref, recv, wts, turned, acts,
    sendp, recvp, own_half, sib_send, sib_recv, ret, back, outs, outq, frame_out,
    w_sem, loc_sem, d_send, d_recv, s_send, s_recv, p_send, p_recv,
    h_send, h_recv, r_send, r_recv, rl_sem, q_send, q_recv, o_sem, f_sem,
):
    e = lax.axis_index("expert")
    c = lax.axis_index("etp")
    z = lax.axis_index("dp")
    ex, ey = e // 4, lax.rem(e, 4)
    p = z + 1 - 2 * lax.rem(z, 2)
    q = 3 - z
    o = 3 - p
    own = z // 2
    plane = (z, q)
    out_refs = (og_ref, ou_ref, od_ref)

    barrier = pltpu.get_barrier_semaphore()

    def greet(i, _):
        d = lax.rem(e + i, PEERS)
        pl.semaphore_signal(barrier, inc=1, device_id=(d, c, q), device_id_type=MESH)

        @pl.when(i > 0)
        def _():
            pl.semaphore_signal(barrier, inc=1, device_id=(d, c, z), device_id_type=MESH)

        return 0

    lax.fori_loop(0, PEERS, greet, 0)
    pl.semaphore_signal(barrier, inc=1, device_id=(e, c, p), device_id_type=MESH)
    pl.semaphore_signal(barrier, inc=1, device_id=(e, 1 - c, z), device_id_type=MESH)

    wcopy = [
        pltpu.make_async_copy(w.at[own], wts.at[i], w_sem.at[i])
        for i, w in enumerate((wg_hbm, wu_hbm, wd_hbm))
    ]
    for w in wcopy:
        w.start()

    ids = lax.broadcasted_iota(jnp.int32, (EXPERTS, TOK), 0)
    first = ids == routes_ref[0:1, :]
    second = ids == routes_ref[1:2, :]
    named = first | second
    before = lax.broadcasted_iota(jnp.int32, (TOK, TOK), 0) < lax.broadcasted_iota(
        jnp.int32, (TOK, TOK), 1
    )
    count = jnp.dot(
        named.astype(F32).astype(BF), before.astype(F32).astype(BF), preferred_element_type=F32
    )
    place_ref[...] = jnp.where(named, count, -1.0)
    level = jnp.where(first, levels_ref[0:1, :], levels_ref[1:2, :])
    gate_ref[...] = level.astype(F32) / 256.0
    slots = lax.broadcasted_iota(jnp.int32, (CAP, TOK), 0).astype(F32)

    def at(dx, dy):
        return lax.rem(ex + dx, 4) * 4 + lax.rem(ey + dy, 4)

    def rows_of(i):
        return pl.ds(i * CAP if isinstance(i, int) else pl.multiple_of(i * CAP, CAP), CAP)

    def group_rows(g):
        return pl.ds(g * RB if isinstance(g, int) else pl.multiple_of(g * RB, RB), RB)

    def pack(g):
        for j in range(GROUP):
            dx, dy, k = BLOCKS[g * GROUP + j]
            expert = 2 * at(dx, dy) + (own if k == 0 else 1 - own)
            hit = place_ref[pl.ds(expert, 1), :] == slots
            pick_ref[rows_of(j), :] = jnp.where(hit, 1.0, 0.0).astype(BF)
            scaled_ref[rows_of(j), :] = jnp.where(hit, gate_ref[pl.ds(expert, 1), :], 0.0).astype(BF)
        rows = group_rows(g)
        send_ref[rows, 0:HALF] = jnp.dot(
            pick_ref[...], frames_ref[...], preferred_element_type=F32
        ).astype(BF)
        send_ref[rows, HALF : 2 * HALF] = jnp.dot(
            scaled_ref[...], grads_ref[...], preferred_element_type=F32
        ).astype(BF)

    def choose(a, b):
        return a if a == b else jnp.where(c == 0, a, b)

    def give(t):
        one, two = SENDS[0][t], SENDS[1][t]
        dx, dy, k, i = [
            choose(a, b) for a, b in zip(one + (INDEX[one],), two + (INDEX[two],))
        ]
        return pltpu.make_async_remote_copy(
            src_ref=send_ref.at[rows_of(i)],
            dst_ref=recv.at[c, rows_of(i)],
            send_sem=d_send.at[i],
            recv_sem=d_recv.at[i],
            device_id=(at(dx, dy), c, jnp.where(k == 0, z, q)),
            device_id_type=MESH,
        )

    def take(i):
        return pltpu.make_async_remote_copy(
            src_ref=send_ref.at[rows_of(i)],
            dst_ref=recv.at[c, rows_of(i)],
            send_sem=d_send.at[i],
            recv_sem=d_recv.at[i],
            device_id=(e, c, q),
            device_id_type=MESH,
        )

    def share(half, i):
        return pltpu.make_async_remote_copy(
            src_ref=recv.at[half, rows_of(i)],
            dst_ref=recv.at[half, rows_of(i)],
            send_sem=s_send.at[i],
            recv_sem=s_recv.at[i],
            device_id=(e, 1 - c, z),
            device_id_type=MESH,
        )

    local = pltpu.make_async_copy(send_ref.at[rows_of(0)], recv.at[c, rows_of(0)], loc_sem)
    for g in range(4):
        pack(g)
        if g == 0:
            pl.semaphore_wait(barrier, 2 * PEERS + 1)
            local.start()
        for t in range(g * GROUP, (g + 1) * GROUP):
            if SENDS[0][t] == (0, 0, 0):
                pl.when(c == 1)(lambda t=t: give(t).start())
            elif SENDS[1][t] == (0, 0, 0):
                pl.when(c == 0)(lambda t=t: give(t).start())
            else:
                give(t).start()
    for w in wcopy:
        w.wait()

    def arrive(g):
        for i in range(g * GROUP, (g + 1) * GROUP):
            if i == 0:
                local.wait()
            else:
                take(i).wait_recv()
            share(c, i).start()

        def mate(j, _):
            share(1 - c, g * GROUP + j).wait_recv()
            return 0

        lax.fori_loop(0, GROUP, mate, 0)

    def forward(g, ch):
        rows = group_rows(g)
        cols = pl.ds(pl.multiple_of(ch * CH, CH), CH)

        def product(i, base):
            total = jnp.dot(
                recv[0, rows, base : base + HALF], wts[i, 0:HALF, cols], preferred_element_type=F32
            )
            return total + jnp.dot(
                recv[1, rows, base : base + HALF], wts[i, HALF:D, cols], preferred_element_type=F32
            )

        pre_gate = product(0, 0)
        pre_up = product(1, 0)
        sig = jax.nn.sigmoid(pre_gate)
        act = pre_gate * sig
        acts[2, ch, rows, :] = (act * pre_up).astype(BF)
        grad = product(2, HALF)
        acts[0, ch, rows, :] = (
            grad * pre_up * sig * (1.0 + pre_gate * (1.0 - sig))
        ).astype(BF)
        acts[1, ch, rows, :] = (grad * act).astype(BF)

    def turn(g):
        rows = group_rows(g)

        def body(half, _):
            for t in range(2):
                for h in range(2):
                    base = t * HALF + h * SL
                    turned[t, 2 * half + h, :, rows] = recv[half, rows, base : base + SL].T
            return 0

        lax.fori_loop(0, 2, body, 0)

    def early(i, _):
        forward(i // NCH, lax.rem(i, NCH))
        return 0

    for g in range(4):
        arrive(g)
        turn(g)
        if g < 2:
            lax.fori_loop(g * NCH, (g + 1) * NCH, early, 0)

    def to_mate(ch, m, i):
        return pltpu.make_async_remote_copy(
            src_ref=sendp.at[i, ch, m],
            dst_ref=recvp.at[i, ch, m],
            send_sem=p_send.at[i, ch, m],
            recv_sem=p_recv.at[i, ch, m],
            device_id=(e, c, p),
            device_id_type=MESH,
        )

    def weight_grad(m, ch, part):
        lhs = turned[0 if m < 2 else 1, part]
        return jnp.dot(lhs, acts[m, ch], preferred_element_type=F32)

    def beyond(ch, _):
        def rest(g, _):
            forward(g, ch)
            return 0

        lax.fori_loop(2, 4, rest, 0)
        for m in range(3):
            sendp[0, ch, m] = weight_grad(m, ch, o).astype(BF)
            to_mate(ch, m, 0).start()
        return 0

    lax.fori_loop(0, NCH, beyond, 0)

    def swap(b):
        return pltpu.make_async_remote_copy(
            src_ref=sib_send.at[b],
            dst_ref=sib_recv.at[b],
            send_sem=h_send.at[b],
            recv_sem=h_recv.at[b],
            device_id=(e, 1 - c, z),
            device_id_type=MESH,
        )

    def input_grad(b, _):
        rows = group_rows(b)

        def half_of(h):
            feats = pl.ds(pl.multiple_of(h * HALF, HALF), HALF)
            total = jnp.zeros((RB, HALF), F32)
            for w in range(2):
                for ch in range(NCH):
                    total += lax.dot_general(
                        acts[w, ch, rows, :],
                        wts[w, feats, ch * CH : (ch + 1) * CH],
                        (((1,), (1,)), ((), ())),
                        preferred_element_type=F32,
                    )
            return total

        sib_send[b] = half_of(1 - c).astype(BF)
        swap(b).start()
        own_half[b] = half_of(c)
        return 0

    lax.fori_loop(0, 4, input_grad, 0)

    def ending(ch, _):
        for m in range(3):
            sendp[1, ch, m] = weight_grad(m, ch, p).astype(BF)
            to_mate(ch, m, 1).start()
        return 0

    lax.fori_loop(0, NCH, ending, 0)

    def give_back(i):
        dx, dy, k = BLOCKS[i]
        return pltpu.make_async_remote_copy(
            src_ref=ret.at[rows_of(i)],
            dst_ref=back.at[e, own],
            send_sem=r_send.at[i],
            recv_sem=r_recv.at[k, e],
            device_id=(at((4 - dx) % 4, (4 - dy) % 4), c, plane[k]),
            device_id_type=MESH,
        )

    def take_back(s, k):
        return pltpu.make_async_remote_copy(
            src_ref=ret.at[rows_of(0)],
            dst_ref=back.at[s, own if k == 0 else 1 - own],
            send_sem=r_send.at[0],
            recv_sem=r_recv.at[k, s],
            device_id=(s, c, plane[k]),
            device_id_type=MESH,
        )

    back_local = pltpu.make_async_copy(ret.at[rows_of(0)], back.at[e, own], rl_sem)
    for b in range(4):
        swap(b).wait_recv()
        ret[group_rows(b), :] = (own_half[b] + sib_recv[b].astype(F32)).astype(BF)
        for i in range(b * GROUP, (b + 1) * GROUP):
            if i == 0:
                back_local.start()
            else:
                give_back(i).start()

    def place_of(ch, m, expert):
        return out_refs[m].at[expert, :, pl.ds(pl.multiple_of(ch * CH, CH), CH)]

    def with_q(ch, m, expert):
        return pltpu.make_async_remote_copy(
            src_ref=outq.at[ch, m],
            dst_ref=place_of(ch, m, expert),
            send_sem=q_send.at[ch, m],
            recv_sem=q_recv.at[ch, m],
            device_id=(e, c, q),
            device_id_type=MESH,
        )

    def to_out(ch, m):
        return pltpu.make_async_copy(outs.at[ch, m], place_of(ch, m, own), o_sem.at[ch, m])

    def pass_on(ch, _):
        for m in range(3):
            total = weight_grad(m, ch, q)
            to_mate(ch, m, 0).wait_recv()
            outq[ch, m] = (total + recvp[0, ch, m].astype(F32)).astype(BF)
            with_q(ch, m, own).start()
        return 0

    lax.fori_loop(0, NCH, pass_on, 0)

    def finish(ch, _):
        for m in range(3):
            total = weight_grad(m, ch, z)
            to_mate(ch, m, 1).wait_recv()
            outs[ch, m] = (total + recvp[1, ch, m].astype(F32)).astype(BF)
            to_out(ch, m).start()
        return 0

    lax.fori_loop(0, NCH // 2, finish, 0)

    def drain_back(i, _):
        take_back(i, 1).wait_recv()

        @pl.when(i != e)
        def _():
            take_back(i, 0).wait_recv()

        return 0

    lax.fori_loop(0, PEERS, drain_back, 0)
    back_local.wait()
    total = jnp.zeros((TOK, HALF), F32)
    step = 8
    for g in range(EXPERTS // step):
        parts = []
        for j in range(step):
            x = g * step + j
            parts.append(jnp.where(place_ref[x : x + 1, :] == slots, 1.0, 0.0).astype(BF))
        pick = jnp.concatenate(parts, axis=0)
        rows = back[g * step // 2 : (g + 1) * step // 2].reshape(step * CAP, HALF)
        total += jnp.dot(pick.T, rows, preferred_element_type=F32)
    frame_out[...] = total.astype(BF)
    frame_copy = pltpu.make_async_copy(frame_out, frame_ref, f_sem)
    frame_copy.start()

    lax.fori_loop(NCH // 2, NCH, finish, 0)

    def drain_blocks(i, _):
        share(c, i).wait_send()

        @pl.when(i > 0)
        def _():
            take(i).wait_send()
            pltpu.make_async_remote_copy(
                src_ref=ret.at[rows_of(i)],
                dst_ref=back.at[e, own],
                send_sem=r_send.at[i],
                recv_sem=r_recv.at[0, e],
                device_id=(e, c, q),
                device_id_type=MESH,
            ).wait_send()

        return 0

    lax.fori_loop(0, NBLOCK, drain_blocks, 0)
    frame_copy.wait()

    def drain(ch, _):
        swap(ch).wait_send()
        for m in range(3):
            for i in range(2):
                to_mate(ch, m, i).wait_send()
            with_q(ch, m, own).wait_send()
            with_q(ch, m, 1 - own).wait_recv()
            to_out(ch, m).wait()
        return 0

    lax.fori_loop(0, NCH, drain, 0)


def layer(routes, levels, frames, out_grad, w_gate, w_up, w_down):
    dma = pltpu.SemaphoreType.DMA
    grad = jax.ShapeDtypeStruct((2, SL, FF), BF)
    return pl.pallas_call(
        layer_kernel,
        out_shape=[grad, grad, grad, jax.ShapeDtypeStruct((TOK, HALF), BF)],
        in_specs=[VM] * 4 + [ANY] * 3,
        out_specs=[ANY] * 4,
        scratch_shapes=[
            pltpu.VMEM((EXPERTS, TOK), F32),
            pltpu.VMEM((EXPERTS, TOK), F32),
            pltpu.VMEM((RB, TOK), BF),
            pltpu.VMEM((RB, TOK), BF),
            pltpu.VMEM((ROWS, 2 * HALF), BF),
            pltpu.VMEM((2, ROWS, 2 * HALF), BF),
            pltpu.VMEM((3, D, FF), BF),
            pltpu.VMEM((2, DP, SL, ROWS), BF),
            pltpu.VMEM((3, NCH, ROWS, CH), BF),
            pltpu.VMEM((2, NCH, 3, SL, CH), BF),
            pltpu.VMEM((2, NCH, 3, SL, CH), BF),
            pltpu.VMEM((4, RB, HALF), F32),
            pltpu.VMEM((4, RB, HALF), BF),
            pltpu.VMEM((4, RB, HALF), BF),
            pltpu.VMEM((ROWS, HALF), BF),
            pltpu.VMEM((PEERS, 2, CAP, HALF), BF),
            pltpu.VMEM((NCH, 3, SL, CH), BF),
            pltpu.VMEM((NCH, 3, SL, CH), BF),
            pltpu.VMEM((TOK, HALF), BF),
            dma((3,)),
            dma,
            dma((NBLOCK,)),
            dma((NBLOCK,)),
            dma((NBLOCK,)),
            dma((NBLOCK,)),
            dma((2, NCH, 3)),
            dma((2, NCH, 3)),
            dma((4,)),
            dma((4,)),
            dma((NBLOCK,)),
            dma((2, PEERS)),
            dma,
            dma((NCH, 3)),
            dma((NCH, 3)),
            dma((NCH, 3)),
            dma,
        ],
        compiler_params=pltpu.CompilerParams(
            collective_id=1, has_side_effects=True, vmem_limit_bytes=60 * 1024 * 1024
        ),
        cost_estimate=pl.CostEstimate(
            flops=16 * ROWS * D * FF, bytes_accessed=20_000_000, transcendentals=ROWS * FF
        ),
        name="layer",
    )(routes, levels, frames, out_grad, w_gate, w_up, w_down)


def settle_kernel(*refs):
    n = (len(refs) - 2) // 3
    ins, outs, held = refs[:n], refs[n : 2 * n], refs[2 * n : 3 * n]
    in_sem, out_sem = refs[3 * n :]
    pieces = []
    for i in range(n):
        half = ins[i].shape[0] // 2
        for j in range(2):
            part = pl.ds(j * half, half)
            pieces.append(
                (
                    pltpu.make_async_copy(ins[i].at[part], held[i].at[part], in_sem.at[i, j]),
                    pltpu.make_async_copy(held[i].at[part], outs[i].at[part], out_sem.at[i, j]),
                )
            )
    for load, _ in pieces:
        load.start()
    for load, store in pieces:
        load.wait()
        store.start()
    for _, store in pieces:
        store.wait()


def settle(*arrays):
    n = len(arrays)
    return pl.pallas_call(
        settle_kernel,
        out_shape=[jax.ShapeDtypeStruct(a.shape, a.dtype) for a in arrays],
        in_specs=[ANY] * n,
        out_specs=[ANY] * n,
        scratch_shapes=[pltpu.VMEM(a.shape, a.dtype) for a in arrays]
        + [pltpu.SemaphoreType.DMA((n, 2))] * 2,
        name="settle",
    )(*arrays)


def local(frames, out_grad, routes, gate_levels, w_gate, w_up, w_down):
    gate_grad, up_grad, down_grad, frame_grad = settle(
        *layer(routes.T, gate_levels.T, frames, out_grad, w_gate, w_up, w_down)
    )
    return frame_grad, gate_grad, up_grad, down_grad


def solution(mesh):
    placed = (
        P(("expert", "dp"), "etp"),
        P(("expert", "dp"), "etp"),
        P(("expert", "dp"), None),
        P(("expert", "dp"), None),
        P("expert", None, "etp"),
        P("expert", None, "etp"),
        P("expert", None, "etp"),
    )
    return jax.shard_map(
        local,
        mesh=mesh,
        in_specs=placed,
        out_specs=(
            P(("expert", "dp"), "etp"),
            P("expert", "dp", "etp"),
            P("expert", "dp", "etp"),
            P("expert", "dp", "etp"),
        ),
        check_vma=False,
    )
```

```python
import jax
import jax.numpy as jnp
from jax import lax
from jax.experimental import pallas as pl
from jax.experimental.pallas import tpu as pltpu
from jax.sharding import PartitionSpec as P

MESH = pl.DeviceIdType.MESH
BF, F32 = jnp.bfloat16, jnp.float32
PEERS, DP = 16, 4
EXPERTS = 32
CAP = 48
TOK = 384
D = 1024
HALF = 512
FF = 1024
ROWS = 2 * PEERS * CAP
CH = 256
NCH = FF // CH
SL = D // DP
RB = 384
ANY = pl.BlockSpec(memory_space=pl.ANY)


def offsets(names):
    kinds = {
        "a": [(1, 0), (3, 0)], "b": [(0, 1), (0, 3)], "c": [(1, 1), (3, 3)], "d": [(1, 3), (3, 1)],
        "e": [(2, 1), (2, 3)], "f": [(1, 2), (3, 2)], "g": [(2, 0)], "h": [(0, 2)], "i": [(2, 2)],
        "l": [(0, 0)],
    }
    return [off for name in names for off in kinds[name]]


def mirrored(off):
    return (4 - off[0]) % 4, (4 - off[1]) % 4


GROUPS = [
    (offsets(here), offsets(there))
    for here, there in zip(("lid", "af", "be", "cgh"), ("be", "dil", "cgh", "af"))
]
BLOCKS = [
    block for here, there in GROUPS for a, b in zip(here, there) for block in (a + (0,), b + (1,))
]
INDEX = {block: i for i, block in enumerate(BLOCKS)}
NBLOCK = len(BLOCKS)
SENDS = [
    BLOCKS,
    [
        block
        for here, there in GROUPS
        for a, b in zip(here, there)
        for block in (mirrored(b) + (1,), mirrored(a) + (0,))
    ],
]
GROUP = NBLOCK // 4


def layer_kernel(
    routes_hbm, levels_hbm, frames_hbm, grads_hbm, wg_hbm, wu_hbm, wd_hbm,
    og_ref, ou_ref, od_ref, frame_ref,
    routes_ref, levels_ref, frames_ref, grads_ref,
    place_ref, gate_ref, pick_ref, scaled_ref, send_ref, recv, wts, turned, acts,
    sendp, recvp, own_half, sib_send, sib_recv, ret, back, outs, outq, frame_out,
    i_sem, w_sem, loc_sem, d_send, d_recv, s_send, s_recv, p_send, p_recv,
    h_send, h_recv, r_send, r_recv, rl_sem, q_send, q_recv, o_sem, f_sem,
):
    e = lax.axis_index("expert")
    c = lax.axis_index("etp")
    z = lax.axis_index("dp")
    ex, ey = e // 4, lax.rem(e, 4)
    p = z + 1 - 2 * lax.rem(z, 2)
    q = 3 - z
    o = 3 - p
    own = z // 2
    plane = (z, q)
    out_refs = (og_ref, ou_ref, od_ref)

    loads = [
        pltpu.make_async_copy(source, target, i_sem.at[i])
        for i, (source, target) in enumerate(
            (
                (routes_hbm, routes_ref),
                (levels_hbm, levels_ref),
                (frames_hbm, frames_ref),
                (grads_hbm, grads_ref),
            )
        )
    ]
    for load in loads:
        load.start()
    barrier = pltpu.get_barrier_semaphore()

    def greet(i, _):
        d = lax.rem(e + i, PEERS)
        pl.semaphore_signal(barrier, inc=1, device_id=(d, c, q), device_id_type=MESH)

        @pl.when(i > 0)
        def _():
            pl.semaphore_signal(barrier, inc=1, device_id=(d, c, z), device_id_type=MESH)

        return 0

    lax.fori_loop(0, PEERS, greet, 0)
    pl.semaphore_signal(barrier, inc=1, device_id=(e, c, p), device_id_type=MESH)
    pl.semaphore_signal(barrier, inc=1, device_id=(e, 1 - c, z), device_id_type=MESH)

    wcopy = [
        pltpu.make_async_copy(w.at[own], wts.at[i], w_sem.at[i])
        for i, w in enumerate((wg_hbm, wu_hbm, wd_hbm))
    ]
    for w in wcopy:
        w.start()

    for load in loads:
        load.wait()

    ids = lax.broadcasted_iota(jnp.int32, (EXPERTS, TOK), 0)
    first = ids == routes_ref[0:1, :]
    second = ids == routes_ref[1:2, :]
    named = first | second
    before = lax.broadcasted_iota(jnp.int32, (TOK, TOK), 0) < lax.broadcasted_iota(
        jnp.int32, (TOK, TOK), 1
    )
    count = jnp.dot(
        named.astype(F32).astype(BF), before.astype(F32).astype(BF), preferred_element_type=F32
    )
    place_ref[...] = jnp.where(named, count, -1.0)
    level = jnp.where(first, levels_ref[0:1, :], levels_ref[1:2, :])
    gate_ref[...] = level.astype(F32) / 256.0
    slots = lax.broadcasted_iota(jnp.int32, (CAP, TOK), 0).astype(F32)

    def at(dx, dy):
        return lax.rem(ex + dx, 4) * 4 + lax.rem(ey + dy, 4)

    def rows_of(i):
        return pl.ds(i * CAP if isinstance(i, int) else pl.multiple_of(i * CAP, CAP), CAP)

    def group_rows(g):
        return pl.ds(g * RB if isinstance(g, int) else pl.multiple_of(g * RB, RB), RB)

    def pack(g):
        for j in range(GROUP):
            dx, dy, k = BLOCKS[g * GROUP + j]
            expert = 2 * at(dx, dy) + (own if k == 0 else 1 - own)
            hit = place_ref[pl.ds(expert, 1), :] == slots
            pick_ref[rows_of(j), :] = jnp.where(hit, 1.0, 0.0).astype(BF)
            scaled_ref[rows_of(j), :] = jnp.where(hit, gate_ref[pl.ds(expert, 1), :], 0.0).astype(BF)
        rows = group_rows(g)
        send_ref[rows, 0:HALF] = jnp.dot(
            pick_ref[...], frames_ref[...], preferred_element_type=F32
        ).astype(BF)
        send_ref[rows, HALF : 2 * HALF] = jnp.dot(
            scaled_ref[...], grads_ref[...], preferred_element_type=F32
        ).astype(BF)

    def choose(a, b):
        return a if a == b else jnp.where(c == 0, a, b)

    def give(t):
        one, two = SENDS[0][t], SENDS[1][t]
        dx, dy, k, i = [
            choose(a, b) for a, b in zip(one + (INDEX[one],), two + (INDEX[two],))
        ]
        return pltpu.make_async_remote_copy(
            src_ref=send_ref.at[rows_of(i)],
            dst_ref=recv.at[c, rows_of(i)],
            send_sem=d_send.at[i],
            recv_sem=d_recv.at[i],
            device_id=(at(dx, dy), c, jnp.where(k == 0, z, q)),
            device_id_type=MESH,
        )

    def take(i):
        return pltpu.make_async_remote_copy(
            src_ref=send_ref.at[rows_of(i)],
            dst_ref=recv.at[c, rows_of(i)],
            send_sem=d_send.at[i],
            recv_sem=d_recv.at[i],
            device_id=(e, c, q),
            device_id_type=MESH,
        )

    def share(half, i):
        return pltpu.make_async_remote_copy(
            src_ref=recv.at[half, rows_of(i)],
            dst_ref=recv.at[half, rows_of(i)],
            send_sem=s_send.at[i],
            recv_sem=s_recv.at[i],
            device_id=(e, 1 - c, z),
            device_id_type=MESH,
        )

    local = pltpu.make_async_copy(send_ref.at[rows_of(0)], recv.at[c, rows_of(0)], loc_sem)
    for g in range(4):
        pack(g)
        if g == 0:
            pl.semaphore_wait(barrier, 2 * PEERS + 1)
            local.start()
        for t in range(g * GROUP, (g + 1) * GROUP):
            if SENDS[0][t] == (0, 0, 0):
                pl.when(c == 1)(lambda t=t: give(t).start())
            elif SENDS[1][t] == (0, 0, 0):
                pl.when(c == 0)(lambda t=t: give(t).start())
            else:
                give(t).start()
    for w in wcopy:
        w.wait()

    def arrive(g):
        for i in range(g * GROUP, (g + 1) * GROUP):
            if i == 0:
                local.wait()
            else:
                take(i).wait_recv()
            share(c, i).start()

        def mate(j, _):
            share(1 - c, g * GROUP + j).wait_recv()
            return 0

        lax.fori_loop(0, GROUP, mate, 0)

    def forward(g, ch):
        rows = group_rows(g)
        cols = pl.ds(pl.multiple_of(ch * CH, CH), CH)

        def product(i, base):
            total = jnp.dot(
                recv[0, rows, base : base + HALF], wts[i, 0:HALF, cols], preferred_element_type=F32
            )
            return total + jnp.dot(
                recv[1, rows, base : base + HALF], wts[i, HALF:D, cols], preferred_element_type=F32
            )

        pre_gate = product(0, 0)
        pre_up = product(1, 0)
        sig = jax.nn.sigmoid(pre_gate)
        act = pre_gate * sig
        acts[2, ch, rows, :] = (act * pre_up).astype(BF)
        grad = product(2, HALF)
        acts[0, ch, rows, :] = (
            grad * pre_up * sig * (1.0 + pre_gate * (1.0 - sig))
        ).astype(BF)
        acts[1, ch, rows, :] = (grad * act).astype(BF)

    def turn(g):
        rows = group_rows(g)

        def body(half, _):
            for t in range(2):
                for h in range(2):
                    base = t * HALF + h * SL
                    turned[t, 2 * half + h, :, rows] = recv[half, rows, base : base + SL].T
            return 0

        lax.fori_loop(0, 2, body, 0)

    def early(i, _):
        forward(i // NCH, lax.rem(i, NCH))
        return 0

    for g in range(4):
        arrive(g)
        turn(g)
        if g < 3:
            lax.fori_loop(g * NCH, (g + 1) * NCH, early, 0)

    def to_mate(ch, m, i):
        return pltpu.make_async_remote_copy(
            src_ref=sendp.at[i, ch, m],
            dst_ref=recvp.at[i, ch, m],
            send_sem=p_send.at[i, ch, m],
            recv_sem=p_recv.at[i, ch, m],
            device_id=(e, c, p),
            device_id_type=MESH,
        )

    def weight_grad(m, ch, part):
        lhs = turned[0 if m < 2 else 1, part]
        return jnp.dot(lhs, acts[m, ch], preferred_element_type=F32)

    def beyond(ch, _):
        def rest(g, _):
            forward(g, ch)
            return 0

        lax.fori_loop(3, 4, rest, 0)
        for m in range(3):
            sendp[0, ch, m] = weight_grad(m, ch, o).astype(BF)
            to_mate(ch, m, 0).start()
        return 0

    lax.fori_loop(0, NCH, beyond, 0)

    def swap(b):
        return pltpu.make_async_remote_copy(
            src_ref=sib_send.at[b],
            dst_ref=sib_recv.at[b],
            send_sem=h_send.at[b],
            recv_sem=h_recv.at[b],
            device_id=(e, 1 - c, z),
            device_id_type=MESH,
        )

    def input_grad(b, _):
        rows = group_rows(b)

        def half_of(h):
            feats = pl.ds(pl.multiple_of(h * HALF, HALF), HALF)
            total = jnp.zeros((RB, HALF), F32)
            for w in range(2):
                for ch in range(NCH):
                    total += lax.dot_general(
                        acts[w, ch, rows, :],
                        wts[w, feats, ch * CH : (ch + 1) * CH],
                        (((1,), (1,)), ((), ())),
                        preferred_element_type=F32,
                    )
            return total

        sib_send[b] = half_of(1 - c).astype(BF)
        swap(b).start()
        own_half[b] = half_of(c)
        return 0

    lax.fori_loop(0, 4, input_grad, 0)

    def ending(ch, _):
        for m in range(3):
            sendp[1, ch, m] = weight_grad(m, ch, p).astype(BF)
            to_mate(ch, m, 1).start()
        return 0


    def give_back(i):
        dx, dy, k = BLOCKS[i]
        return pltpu.make_async_remote_copy(
            src_ref=ret.at[rows_of(i)],
            dst_ref=back.at[e, own],
            send_sem=r_send.at[i],
            recv_sem=r_recv.at[k, e],
            device_id=(at((4 - dx) % 4, (4 - dy) % 4), c, plane[k]),
            device_id_type=MESH,
        )

    def take_back(s, k):
        return pltpu.make_async_remote_copy(
            src_ref=ret.at[rows_of(0)],
            dst_ref=back.at[s, own if k == 0 else 1 - own],
            send_sem=r_send.at[0],
            recv_sem=r_recv.at[k, s],
            device_id=(s, c, plane[k]),
            device_id_type=MESH,
        )

    back_local = pltpu.make_async_copy(ret.at[rows_of(0)], back.at[e, own], rl_sem)
    for b in range(4):
        swap(b).wait_recv()
        ret[group_rows(b), :] = (own_half[b] + sib_recv[b].astype(F32)).astype(BF)
        for i in range(b * GROUP, (b + 1) * GROUP):
            if i == 0:
                back_local.start()
            else:
                give_back(i).start()

    lax.fori_loop(0, NCH, ending, 0)

    def place_of(ch, m, expert):
        return out_refs[m].at[expert, :, pl.ds(pl.multiple_of(ch * CH, CH), CH)]

    def with_q(ch, m, expert):
        return pltpu.make_async_remote_copy(
            src_ref=outq.at[ch, m],
            dst_ref=place_of(ch, m, expert),
            send_sem=q_send.at[ch, m],
            recv_sem=q_recv.at[ch, m],
            device_id=(e, c, q),
            device_id_type=MESH,
        )

    def to_out(ch, m):
        return pltpu.make_async_copy(outs.at[ch, m], place_of(ch, m, own), o_sem.at[ch, m])

    def pass_on(ch, _):
        for m in range(3):
            total = weight_grad(m, ch, q)
            to_mate(ch, m, 0).wait_recv()
            outq[ch, m] = (total + recvp[0, ch, m].astype(F32)).astype(BF)
            with_q(ch, m, own).start()
        return 0

    lax.fori_loop(0, NCH, pass_on, 0)

    def finish(ch, _):
        for m in range(3):
            total = weight_grad(m, ch, z)
            to_mate(ch, m, 1).wait_recv()
            outs[ch, m] = (total + recvp[1, ch, m].astype(F32)).astype(BF)
            to_out(ch, m).start()
        return 0

    lax.fori_loop(0, NCH // 2, finish, 0)

    def drain_back(i, _):
        take_back(i, 1).wait_recv()

        @pl.when(i != e)
        def _():
            take_back(i, 0).wait_recv()

        return 0

    lax.fori_loop(0, PEERS, drain_back, 0)
    back_local.wait()
    total = jnp.zeros((TOK, HALF), F32)
    step = 8
    for g in range(EXPERTS // step):
        parts = []
        for j in range(step):
            x = g * step + j
            parts.append(jnp.where(place_ref[x : x + 1, :] == slots, 1.0, 0.0).astype(BF))
        pick = jnp.concatenate(parts, axis=0)
        rows = back[g * step // 2 : (g + 1) * step // 2].reshape(step * CAP, HALF)
        total += jnp.dot(pick.T, rows, preferred_element_type=F32)
    frame_out[...] = total.astype(BF)
    frame_copy = pltpu.make_async_copy(frame_out, frame_ref, f_sem)
    frame_copy.start()

    lax.fori_loop(NCH // 2, NCH, finish, 0)

    def drain_blocks(i, _):
        share(c, i).wait_send()

        @pl.when(i > 0)
        def _():
            take(i).wait_send()
            pltpu.make_async_remote_copy(
                src_ref=ret.at[rows_of(i)],
                dst_ref=back.at[e, own],
                send_sem=r_send.at[i],
                recv_sem=r_recv.at[0, e],
                device_id=(e, c, q),
                device_id_type=MESH,
            ).wait_send()

        return 0

    lax.fori_loop(0, NBLOCK, drain_blocks, 0)
    frame_copy.wait()

    def drain(ch, _):
        swap(ch).wait_send()
        for m in range(3):
            for i in range(2):
                to_mate(ch, m, i).wait_send()
            with_q(ch, m, own).wait_send()
            with_q(ch, m, 1 - own).wait_recv()
            to_out(ch, m).wait()
        return 0

    lax.fori_loop(0, NCH, drain, 0)


def layer(routes, levels, frames, out_grad, w_gate, w_up, w_down):
    dma = pltpu.SemaphoreType.DMA
    grad = jax.ShapeDtypeStruct((2, SL, FF), BF)
    return pl.pallas_call(
        layer_kernel,
        out_shape=[grad, grad, grad, jax.ShapeDtypeStruct((TOK, HALF), BF)],
        in_specs=[ANY] * 7,
        out_specs=[ANY] * 4,
        scratch_shapes=[
            pltpu.VMEM((2, TOK), jnp.int32),
            pltpu.VMEM((2, TOK), jnp.int32),
            pltpu.VMEM((TOK, HALF), BF),
            pltpu.VMEM((TOK, HALF), BF),
            pltpu.VMEM((EXPERTS, TOK), F32),
            pltpu.VMEM((EXPERTS, TOK), F32),
            pltpu.VMEM((RB, TOK), BF),
            pltpu.VMEM((RB, TOK), BF),
            pltpu.VMEM((ROWS, 2 * HALF), BF),
            pltpu.VMEM((2, ROWS, 2 * HALF), BF),
            pltpu.VMEM((3, D, FF), BF),
            pltpu.VMEM((2, DP, SL, ROWS), BF),
            pltpu.VMEM((3, NCH, ROWS, CH), BF),
            pltpu.VMEM((2, NCH, 3, SL, CH), BF),
            pltpu.VMEM((2, NCH, 3, SL, CH), BF),
            pltpu.VMEM((4, RB, HALF), F32),
            pltpu.VMEM((4, RB, HALF), BF),
            pltpu.VMEM((4, RB, HALF), BF),
            pltpu.VMEM((ROWS, HALF), BF),
            pltpu.VMEM((PEERS, 2, CAP, HALF), BF),
            pltpu.VMEM((NCH, 3, SL, CH), BF),
            pltpu.VMEM((NCH, 3, SL, CH), BF),
            pltpu.VMEM((TOK, HALF), BF),
            dma((4,)),
            dma((3,)),
            dma,
            dma((NBLOCK,)),
            dma((NBLOCK,)),
            dma((NBLOCK,)),
            dma((NBLOCK,)),
            dma((2, NCH, 3)),
            dma((2, NCH, 3)),
            dma((4,)),
            dma((4,)),
            dma((NBLOCK,)),
            dma((2, PEERS)),
            dma,
            dma((NCH, 3)),
            dma((NCH, 3)),
            dma((NCH, 3)),
            dma,
        ],
        compiler_params=pltpu.CompilerParams(
            collective_id=1, has_side_effects=True, vmem_limit_bytes=60 * 1024 * 1024
        ),
        cost_estimate=pl.CostEstimate(
            flops=16 * ROWS * D * FF, bytes_accessed=20_000_000, transcendentals=ROWS * FF
        ),
        name="layer",
    )(routes, levels, frames, out_grad, w_gate, w_up, w_down)


def settle_kernel(*refs):
    n = (len(refs) - 2) // 3
    ins, outs, held = refs[:n], refs[n : 2 * n], refs[2 * n : 3 * n]
    in_sem, out_sem = refs[3 * n :]
    pieces = []
    for i in range(n):
        half = ins[i].shape[0] // 2
        for j in range(2):
            part = pl.ds(j * half, half)
            pieces.append(
                (
                    pltpu.make_async_copy(ins[i].at[part], held[i].at[part], in_sem.at[i, j]),
                    pltpu.make_async_copy(held[i].at[part], outs[i].at[part], out_sem.at[i, j]),
                )
            )
    for load, _ in pieces:
        load.start()
    for load, store in pieces:
        load.wait()
        store.start()
    for _, store in pieces:
        store.wait()


def settle(*arrays):
    n = len(arrays)
    return pl.pallas_call(
        settle_kernel,
        out_shape=[jax.ShapeDtypeStruct(a.shape, a.dtype) for a in arrays],
        in_specs=[ANY] * n,
        out_specs=[ANY] * n,
        scratch_shapes=[pltpu.VMEM(a.shape, a.dtype) for a in arrays]
        + [pltpu.SemaphoreType.DMA((n, 2))] * 2,
        name="settle",
    )(*arrays)


def local(frames, out_grad, routes, gate_levels, w_gate, w_up, w_down):
    gate_grad, up_grad, down_grad, frame_grad = settle(
        *layer(routes.T, gate_levels.T, frames, out_grad, w_gate, w_up, w_down)
    )
    return frame_grad, gate_grad, up_grad, down_grad


def solution(mesh):
    placed = (
        P(("expert", "dp"), "etp"),
        P(("expert", "dp"), "etp"),
        P(("expert", "dp"), None),
        P(("expert", "dp"), None),
        P("expert", None, "etp"),
        P("expert", None, "etp"),
        P("expert", None, "etp"),
    )
    return jax.shard_map(
        local,
        mesh=mesh,
        in_specs=placed,
        out_specs=(
            P(("expert", "dp"), "etp"),
            P("expert", "dp", "etp"),
            P("expert", "dp", "etp"),
            P("expert", "dp", "etp"),
        ),
        check_vma=False,
    )
```

```python
import jax
import jax.numpy as jnp
from jax import lax
from jax.experimental import pallas as pl
from jax.experimental.pallas import tpu as pltpu
from jax.sharding import PartitionSpec as P

MESH = pl.DeviceIdType.MESH
BF, F32 = jnp.bfloat16, jnp.float32
PEERS, DP = 16, 4
EXPERTS = 32
CAP = 48
TOK = 384
D = 1024
HALF = 512
FF = 1024
ROWS = 2 * PEERS * CAP
CH = 256
NCH = FF // CH
SL = D // DP
RB = 384
ANY = pl.BlockSpec(memory_space=pl.ANY)


def offsets(names):
    kinds = {
        "a": [(1, 0), (3, 0)], "b": [(0, 1), (0, 3)], "c": [(1, 1), (3, 3)], "d": [(1, 3), (3, 1)],
        "e": [(2, 1), (2, 3)], "f": [(1, 2), (3, 2)], "g": [(2, 0)], "h": [(0, 2)], "i": [(2, 2)],
        "l": [(0, 0)],
    }
    return [off for name in names for off in kinds[name]]


def mirrored(off):
    return (4 - off[0]) % 4, (4 - off[1]) % 4


GROUPS = [
    (offsets(here), offsets(there))
    for here, there in zip(("lid", "af", "be", "cgh"), ("be", "dil", "cgh", "af"))
]
BLOCKS = [
    block for here, there in GROUPS for a, b in zip(here, there) for block in (a + (0,), b + (1,))
]
INDEX = {block: i for i, block in enumerate(BLOCKS)}
NBLOCK = len(BLOCKS)
SENDS = [
    BLOCKS,
    [
        block
        for here, there in GROUPS
        for a, b in zip(here, there)
        for block in (mirrored(b) + (1,), mirrored(a) + (0,))
    ],
]
GROUP = NBLOCK // 4
DETOURS = (NCH, 0)


def layer_kernel(
    routes_hbm, levels_hbm, frames_hbm, grads_hbm, wg_hbm, wu_hbm, wd_hbm,
    og_ref, ou_ref, od_ref, frame_ref,
    routes_ref, levels_ref, frames_ref, grads_ref,
    place_ref, gate_ref, pick_ref, scaled_ref, send_ref, recv, wts, turned, acts,
    sendp, recvp, passing, own_half, sib_send, sib_recv, ret, back, outs, outq, frame_out,
    i_sem, w_sem, loc_sem, d_send, d_recv, s_send, s_recv, p_send, p_recv, n_send, n_recv,
    h_send, h_recv, r_send, r_recv, rl_sem, q_send, q_recv, o_sem, f_sem,
):
    e = lax.axis_index("expert")
    c = lax.axis_index("etp")
    z = lax.axis_index("dp")
    ex, ey = e // 4, lax.rem(e, 4)
    odd = lax.rem(ex + ey, 2) == 1
    low, high = z + 1 - 2 * lax.rem(z, 2), 3 - z
    p, q = jnp.where(odd, high, low), jnp.where(odd, low, high)
    o = lax.rem(z + 2, 4)
    here, there = z // 2, lax.rem((z + 1) // 2, 2)
    own, own_flip = jnp.where(odd, there, here), jnp.where(odd, here, there)
    plane = (z, q)
    out_refs = (og_ref, ou_ref, od_ref)

    loads = [
        pltpu.make_async_copy(source, target, i_sem.at[i])
        for i, (source, target) in enumerate(
            (
                (routes_hbm, routes_ref),
                (levels_hbm, levels_ref),
                (frames_hbm, frames_ref),
                (grads_hbm, grads_ref),
            )
        )
    ]
    for load in loads:
        load.start()
    barrier = pltpu.get_barrier_semaphore()

    def at(dx, dy):
        return lax.rem(ex + dx, 4) * 4 + lax.rem(ey + dy, 4)

    def greet(i, _):
        d = lax.rem(e + i, PEERS)
        pl.semaphore_signal(barrier, inc=1, device_id=(d, c, q), device_id_type=MESH)

        @pl.when(i > 0)
        def _():
            pl.semaphore_signal(barrier, inc=1, device_id=(d, c, z), device_id_type=MESH)

        return 0

    lax.fori_loop(0, PEERS, greet, 0)
    for dx in range(4):
        for dy in range(4):
            if (dx + dy) % 2 == 1:
                pl.semaphore_signal(
                    barrier, inc=1, device_id=(at(dx, dy), c, p), device_id_type=MESH
                )
    pl.semaphore_signal(barrier, inc=1, device_id=(e, c, p), device_id_type=MESH)
    pl.semaphore_signal(barrier, inc=1, device_id=(e, 1 - c, z), device_id_type=MESH)

    wcopy = [
        pltpu.make_async_copy(w.at[own], wts.at[i], w_sem.at[i])
        for i, w in enumerate((wg_hbm, wu_hbm, wd_hbm))
    ]
    for w in wcopy:
        w.start()

    for load in loads:
        load.wait()

    ids = lax.broadcasted_iota(jnp.int32, (EXPERTS, TOK), 0)
    first = ids == routes_ref[0:1, :]
    second = ids == routes_ref[1:2, :]
    named = first | second
    before = lax.broadcasted_iota(jnp.int32, (TOK, TOK), 0) < lax.broadcasted_iota(
        jnp.int32, (TOK, TOK), 1
    )
    count = jnp.dot(
        named.astype(F32).astype(BF), before.astype(F32).astype(BF), preferred_element_type=F32
    )
    place_ref[...] = jnp.where(named, count, -1.0)
    level = jnp.where(first, levels_ref[0:1, :], levels_ref[1:2, :])
    gate_ref[...] = level.astype(F32) / 256.0
    slots = lax.broadcasted_iota(jnp.int32, (CAP, TOK), 0).astype(F32)

    def rows_of(i):
        return pl.ds(i * CAP if isinstance(i, int) else pl.multiple_of(i * CAP, CAP), CAP)

    def group_rows(g):
        return pl.ds(g * RB if isinstance(g, int) else pl.multiple_of(g * RB, RB), RB)

    def pack(g):
        for j in range(GROUP):
            dx, dy, k = BLOCKS[g * GROUP + j]
            theirs = own_flip if (dx + dy) % 2 else own
            expert = 2 * at(dx, dy) + (theirs if k == 0 else 1 - theirs)
            hit = place_ref[pl.ds(expert, 1), :] == slots
            pick_ref[rows_of(j), :] = jnp.where(hit, 1.0, 0.0).astype(BF)
            scaled_ref[rows_of(j), :] = jnp.where(hit, gate_ref[pl.ds(expert, 1), :], 0.0).astype(BF)
        rows = group_rows(g)
        send_ref[rows, 0:HALF] = jnp.dot(
            pick_ref[...], frames_ref[...], preferred_element_type=F32
        ).astype(BF)
        send_ref[rows, HALF : 2 * HALF] = jnp.dot(
            scaled_ref[...], grads_ref[...], preferred_element_type=F32
        ).astype(BF)

    def choose(a, b):
        return a if a == b else jnp.where(c == 0, a, b)

    def give(t):
        one, two = SENDS[0][t], SENDS[1][t]
        kinds = [k * (1 + (dx + dy) % 2) for dx, dy, k in (one, two)]
        dx, dy, _, i = [
            choose(a, b) for a, b in zip(one + (INDEX[one],), two + (INDEX[two],))
        ]
        kind = choose(*kinds)
        return pltpu.make_async_remote_copy(
            src_ref=send_ref.at[rows_of(i)],
            dst_ref=recv.at[c, rows_of(i)],
            send_sem=d_send.at[i],
            recv_sem=d_recv.at[i],
            device_id=(at(dx, dy), c, jnp.where(kind == 0, z, jnp.where(kind == 1, q, p))),
            device_id_type=MESH,
        )

    def take(i):
        return pltpu.make_async_remote_copy(
            src_ref=send_ref.at[rows_of(i)],
            dst_ref=recv.at[c, rows_of(i)],
            send_sem=d_send.at[i],
            recv_sem=d_recv.at[i],
            device_id=(e, c, q),
            device_id_type=MESH,
        )

    def share(half, i):
        return pltpu.make_async_remote_copy(
            src_ref=recv.at[half, rows_of(i)],
            dst_ref=recv.at[half, rows_of(i)],
            send_sem=s_send.at[i],
            recv_sem=s_recv.at[i],
            device_id=(e, 1 - c, z),
            device_id_type=MESH,
        )

    local = pltpu.make_async_copy(send_ref.at[rows_of(0)], recv.at[c, rows_of(0)], loc_sem)
    for g in range(4):
        pack(g)
        if g == 0:
            pl.semaphore_wait(barrier, 2 * PEERS + PEERS // 2 + 1)
            local.start()
        for t in range(g * GROUP, (g + 1) * GROUP):
            if SENDS[0][t] == (0, 0, 0):
                pl.when(c == 1)(lambda t=t: give(t).start())
            elif SENDS[1][t] == (0, 0, 0):
                pl.when(c == 0)(lambda t=t: give(t).start())
            else:
                give(t).start()
    for w in wcopy:
        w.wait()

    def arrive(g):
        for i in range(g * GROUP, (g + 1) * GROUP):
            if i == 0:
                local.wait()
            else:
                take(i).wait_recv()
            share(c, i).start()

        def mate(j, _):
            share(1 - c, g * GROUP + j).wait_recv()
            return 0

        lax.fori_loop(0, GROUP, mate, 0)

    def forward(g, ch):
        rows = group_rows(g)
        cols = pl.ds(pl.multiple_of(ch * CH, CH), CH)

        def product(i, base):
            total = jnp.dot(
                recv[0, rows, base : base + HALF], wts[i, 0:HALF, cols], preferred_element_type=F32
            )
            return total + jnp.dot(
                recv[1, rows, base : base + HALF], wts[i, HALF:D, cols], preferred_element_type=F32
            )

        pre_gate = product(0, 0)
        pre_up = product(1, 0)
        sig = jax.nn.sigmoid(pre_gate)
        act = pre_gate * sig
        acts[2, ch, rows, :] = (act * pre_up).astype(BF)
        grad = product(2, HALF)
        acts[0, ch, rows, :] = (
            grad * pre_up * sig * (1.0 + pre_gate * (1.0 - sig))
        ).astype(BF)
        acts[1, ch, rows, :] = (grad * act).astype(BF)

    def turn(g):
        rows = group_rows(g)

        def body(half, _):
            for t in range(2):
                for h in range(2):
                    base = t * HALF + h * SL
                    turned[t, 2 * half + h, :, rows] = recv[half, rows, base : base + SL].T
            return 0

        lax.fori_loop(0, 2, body, 0)

    def early(i, _):
        forward(i // NCH, lax.rem(i, NCH))
        return 0

    for g in range(4):
        arrive(g)
        turn(g)
        if g < 3:
            lax.fori_loop(g * NCH, (g + 1) * NCH, early, 0)

    def to_mate(ch, m, i):
        return pltpu.make_async_remote_copy(
            src_ref=sendp.at[i, ch, m],
            dst_ref=recvp.at[i, ch, m],
            send_sem=p_send.at[i, ch, m],
            recv_sem=p_recv.at[i, ch, m],
            device_id=(e, c, p),
            device_id_type=MESH,
        )

    def to_next(ch, i):
        return pltpu.make_async_remote_copy(
            src_ref=sendp.at[i, ch, 0],
            dst_ref=passing.at[i, ch],
            send_sem=p_send.at[i, ch, 0],
            recv_sem=n_recv.at[i, ch],
            device_id=(at(1, 0), c, p),
            device_id_type=MESH,
        )

    def from_next(ch, i):
        return pltpu.make_async_remote_copy(
            src_ref=passing.at[i, ch],
            dst_ref=recvp.at[i, ch, 0],
            send_sem=n_send.at[i, ch],
            recv_sem=p_recv.at[i, ch, 0],
            device_id=(at(3, 0), c, z),
            device_id_type=MESH,
        )

    def hand_on(i):
        def body(ch, _):
            to_next(ch, i).wait_recv()
            from_next(ch, i).start()
            return 0

        lax.fori_loop(0, DETOURS[i], body, 0)

    def dispatch_slice(ch, m, i):
        if m > 0 or DETOURS[i] == 0:
            to_mate(ch, m, i).start()
        elif DETOURS[i] == NCH:
            to_next(ch, i).start()
        else:
            pl.when(ch < DETOURS[i])(lambda: to_next(ch, i).start())
            pl.when(ch >= DETOURS[i])(lambda: to_mate(ch, m, i).start())

    def weight_grad(m, ch, part):
        lhs = turned[0 if m < 2 else 1, part]
        return jnp.dot(lhs, acts[m, ch], preferred_element_type=F32)

    def beyond(ch, _):
        def rest(g, _):
            forward(g, ch)
            return 0

        lax.fori_loop(3, 4, rest, 0)
        for m in range(3):
            sendp[0, ch, m] = weight_grad(m, ch, o).astype(BF)
            dispatch_slice(ch, m, 0)
        return 0

    lax.fori_loop(0, NCH, beyond, 0)

    def swap(b):
        return pltpu.make_async_remote_copy(
            src_ref=sib_send.at[b],
            dst_ref=sib_recv.at[b],
            send_sem=h_send.at[b],
            recv_sem=h_recv.at[b],
            device_id=(e, 1 - c, z),
            device_id_type=MESH,
        )

    def input_grad(b, _):
        rows = group_rows(b)

        def half_of(h):
            feats = pl.ds(pl.multiple_of(h * HALF, HALF), HALF)
            total = jnp.zeros((RB, HALF), F32)
            for w in range(2):
                for ch in range(NCH):
                    total += lax.dot_general(
                        acts[w, ch, rows, :],
                        wts[w, feats, ch * CH : (ch + 1) * CH],
                        (((1,), (1,)), ((), ())),
                        preferred_element_type=F32,
                    )
            return total

        sib_send[b] = half_of(1 - c).astype(BF)
        swap(b).start()
        own_half[b] = half_of(c)
        return 0

    lax.fori_loop(0, 4, input_grad, 0)
    hand_on(0)

    def ending(ch, _):
        for m in range(3):
            sendp[1, ch, m] = weight_grad(m, ch, p).astype(BF)
            dispatch_slice(ch, m, 1)
        return 0


    def give_back(i):
        dx, dy, k = BLOCKS[i]
        return pltpu.make_async_remote_copy(
            src_ref=ret.at[rows_of(i)],
            dst_ref=back.at[e, own],
            send_sem=r_send.at[i],
            recv_sem=r_recv.at[k, e],
            device_id=(at((4 - dx) % 4, (4 - dy) % 4), c, plane[k]),
            device_id_type=MESH,
        )

    def take_back(s, k):
        alike = lax.rem(s // 4 + lax.rem(s, 4), 2) == lax.rem(ex + ey, 2)
        theirs = jnp.where(alike, own, own_flip)
        return pltpu.make_async_remote_copy(
            src_ref=ret.at[rows_of(0)],
            dst_ref=back.at[s, theirs if k == 0 else 1 - theirs],
            send_sem=r_send.at[0],
            recv_sem=r_recv.at[k, s],
            device_id=(s, c, plane[k]),
            device_id_type=MESH,
        )

    back_local = pltpu.make_async_copy(ret.at[rows_of(0)], back.at[e, own], rl_sem)
    for b in range(4):
        swap(b).wait_recv()
        ret[group_rows(b), :] = (own_half[b] + sib_recv[b].astype(F32)).astype(BF)
        for i in range(b * GROUP, (b + 1) * GROUP):
            if i == 0:
                back_local.start()
            else:
                give_back(i).start()

    lax.fori_loop(0, NCH, ending, 0)

    def place_of(ch, m, expert):
        return out_refs[m].at[expert, :, pl.ds(pl.multiple_of(ch * CH, CH), CH)]

    def with_q(ch, m, expert):
        return pltpu.make_async_remote_copy(
            src_ref=outq.at[ch, m],
            dst_ref=place_of(ch, m, expert),
            send_sem=q_send.at[ch, m],
            recv_sem=q_recv.at[ch, m],
            device_id=(e, c, q),
            device_id_type=MESH,
        )

    def to_out(ch, m):
        return pltpu.make_async_copy(outs.at[ch, m], place_of(ch, m, own), o_sem.at[ch, m])

    def pass_on(ch, _):
        for m in range(3):
            total = weight_grad(m, ch, q)
            to_mate(ch, m, 0).wait_recv()
            outq[ch, m] = (total + recvp[0, ch, m].astype(F32)).astype(BF)
            with_q(ch, m, own).start()
        return 0

    lax.fori_loop(0, NCH, pass_on, 0)
    hand_on(1)

    def finish(ch, _):
        for m in range(3):
            total = weight_grad(m, ch, z)
            to_mate(ch, m, 1).wait_recv()
            outs[ch, m] = (total + recvp[1, ch, m].astype(F32)).astype(BF)
            to_out(ch, m).start()
        return 0

    lax.fori_loop(0, NCH // 2, finish, 0)

    def drain_back(i, _):
        take_back(i, 1).wait_recv()

        @pl.when(i != e)
        def _():
            take_back(i, 0).wait_recv()

        return 0

    lax.fori_loop(0, PEERS, drain_back, 0)
    back_local.wait()
    total = jnp.zeros((TOK, HALF), F32)
    step = 8
    for g in range(EXPERTS // step):
        parts = []
        for j in range(step):
            x = g * step + j
            parts.append(jnp.where(place_ref[x : x + 1, :] == slots, 1.0, 0.0).astype(BF))
        pick = jnp.concatenate(parts, axis=0)
        rows = back[g * step // 2 : (g + 1) * step // 2].reshape(step * CAP, HALF)
        total += jnp.dot(pick.T, rows, preferred_element_type=F32)
    frame_out[...] = total.astype(BF)
    frame_copy = pltpu.make_async_copy(frame_out, frame_ref, f_sem)
    frame_copy.start()

    lax.fori_loop(NCH // 2, NCH, finish, 0)

    def drain_blocks(i, _):
        share(c, i).wait_send()

        @pl.when(i > 0)
        def _():
            take(i).wait_send()
            pltpu.make_async_remote_copy(
                src_ref=ret.at[rows_of(i)],
                dst_ref=back.at[e, own],
                send_sem=r_send.at[i],
                recv_sem=r_recv.at[0, e],
                device_id=(e, c, q),
                device_id_type=MESH,
            ).wait_send()

        return 0

    lax.fori_loop(0, NBLOCK, drain_blocks, 0)
    frame_copy.wait()

    def drain(ch, _):
        swap(ch).wait_send()
        for m in range(3):
            for i in range(2):
                to_mate(ch, m, i).wait_send()
            with_q(ch, m, own).wait_send()
            with_q(ch, m, 1 - own).wait_recv()
            to_out(ch, m).wait()
        return 0

    lax.fori_loop(0, NCH, drain, 0)

    for i in range(2):

        def drain_passing(ch, _, i=i):
            from_next(ch, i).wait_send()
            return 0

        lax.fori_loop(0, DETOURS[i], drain_passing, 0)


def layer(routes, levels, frames, out_grad, w_gate, w_up, w_down):
    dma = pltpu.SemaphoreType.DMA
    grad = jax.ShapeDtypeStruct((2, SL, FF), BF)
    return pl.pallas_call(
        layer_kernel,
        out_shape=[grad, grad, grad, jax.ShapeDtypeStruct((TOK, HALF), BF)],
        in_specs=[ANY] * 7,
        out_specs=[ANY] * 4,
        scratch_shapes=[
            pltpu.VMEM((2, TOK), jnp.int32),
            pltpu.VMEM((2, TOK), jnp.int32),
            pltpu.VMEM((TOK, HALF), BF),
            pltpu.VMEM((TOK, HALF), BF),
            pltpu.VMEM((EXPERTS, TOK), F32),
            pltpu.VMEM((EXPERTS, TOK), F32),
            pltpu.VMEM((RB, TOK), BF),
            pltpu.VMEM((RB, TOK), BF),
            pltpu.VMEM((ROWS, 2 * HALF), BF),
            pltpu.VMEM((2, ROWS, 2 * HALF), BF),
            pltpu.VMEM((3, D, FF), BF),
            pltpu.VMEM((2, DP, SL, ROWS), BF),
            pltpu.VMEM((3, NCH, ROWS, CH), BF),
            pltpu.VMEM((2, NCH, 3, SL, CH), BF),
            pltpu.VMEM((2, NCH, 3, SL, CH), BF),
            pltpu.VMEM((2, NCH, SL, CH), BF),
            pltpu.VMEM((4, RB, HALF), F32),
            pltpu.VMEM((4, RB, HALF), BF),
            pltpu.VMEM((4, RB, HALF), BF),
            pltpu.VMEM((ROWS, HALF), BF),
            pltpu.VMEM((PEERS, 2, CAP, HALF), BF),
            pltpu.VMEM((NCH, 3, SL, CH), BF),
            pltpu.VMEM((NCH, 3, SL, CH), BF),
            pltpu.VMEM((TOK, HALF), BF),
            dma((4,)),
            dma((3,)),
            dma,
            dma((NBLOCK,)),
            dma((NBLOCK,)),
            dma((NBLOCK,)),
            dma((NBLOCK,)),
            dma((2, NCH, 3)),
            dma((2, NCH, 3)),
            dma((2, NCH)),
            dma((2, NCH)),
            dma((4,)),
            dma((4,)),
            dma((NBLOCK,)),
            dma((2, PEERS)),
            dma,
            dma((NCH, 3)),
            dma((NCH, 3)),
            dma((NCH, 3)),
            dma,
        ],
        compiler_params=pltpu.CompilerParams(
            collective_id=1, has_side_effects=True, vmem_limit_bytes=60 * 1024 * 1024
        ),
        cost_estimate=pl.CostEstimate(
            flops=16 * ROWS * D * FF, bytes_accessed=20_000_000, transcendentals=ROWS * FF
        ),
        name="layer",
    )(routes, levels, frames, out_grad, w_gate, w_up, w_down)


def settle_kernel(*refs):
    n = (len(refs) - 2) // 3
    ins, outs, held = refs[:n], refs[n : 2 * n], refs[2 * n : 3 * n]
    in_sem, out_sem = refs[3 * n :]
    pieces = []
    for i in range(n):
        half = ins[i].shape[0] // 2
        for j in range(2):
            part = pl.ds(j * half, half)
            pieces.append(
                (
                    pltpu.make_async_copy(ins[i].at[part], held[i].at[part], in_sem.at[i, j]),
                    pltpu.make_async_copy(held[i].at[part], outs[i].at[part], out_sem.at[i, j]),
                )
            )
    for load, _ in pieces:
        load.start()
    for load, store in pieces:
        load.wait()
        store.start()
    for _, store in pieces:
        store.wait()


def settle(*arrays):
    n = len(arrays)
    return pl.pallas_call(
        settle_kernel,
        out_shape=[jax.ShapeDtypeStruct(a.shape, a.dtype) for a in arrays],
        in_specs=[ANY] * n,
        out_specs=[ANY] * n,
        scratch_shapes=[pltpu.VMEM(a.shape, a.dtype) for a in arrays]
        + [pltpu.SemaphoreType.DMA((n, 2))] * 2,
        name="settle",
    )(*arrays)


def local(frames, out_grad, routes, gate_levels, w_gate, w_up, w_down):
    gate_grad, up_grad, down_grad, frame_grad = settle(
        *layer(routes.T, gate_levels.T, frames, out_grad, w_gate, w_up, w_down)
    )
    return frame_grad, gate_grad, up_grad, down_grad


def solution(mesh):
    placed = (
        P(("expert", "dp"), "etp"),
        P(("expert", "dp"), "etp"),
        P(("expert", "dp"), None),
        P(("expert", "dp"), None),
        P("expert", None, "etp"),
        P("expert", None, "etp"),
        P("expert", None, "etp"),
    )
    return jax.shard_map(
        local,
        mesh=mesh,
        in_specs=placed,
        out_specs=(
            P(("expert", "dp"), "etp"),
            P("expert", "dp", "etp"),
            P("expert", "dp", "etp"),
            P("expert", "dp", "etp"),
        ),
        check_vma=False,
    )
```

```python
import jax
import jax.numpy as jnp
from jax import lax
from jax.experimental import pallas as pl
from jax.experimental.pallas import tpu as pltpu
from jax.sharding import PartitionSpec as P

MESH = pl.DeviceIdType.MESH
BF, F32 = jnp.bfloat16, jnp.float32
PEERS, DP = 16, 4
EXPERTS = 32
CAP = 48
TOK = 384
D = 1024
HALF = 512
FF = 1024
ROWS = 2 * PEERS * CAP
CH = 256
NCH = FF // CH
SL = D // DP
RB = 384
ANY = pl.BlockSpec(memory_space=pl.ANY)


def offsets(names):
    kinds = {
        "a": [(1, 0), (3, 0)], "b": [(0, 1), (0, 3)], "c": [(1, 1), (3, 3)], "d": [(1, 3), (3, 1)],
        "e": [(2, 1), (2, 3)], "f": [(1, 2), (3, 2)], "g": [(2, 0)], "h": [(0, 2)], "i": [(2, 2)],
        "l": [(0, 0)],
    }
    return [off for name in names for off in kinds[name]]


def mirrored(off):
    return (4 - off[0]) % 4, (4 - off[1]) % 4


GROUPS = [
    (offsets(here), offsets(there))
    for here, there in zip(("lid", "af", "be", "cgh"), ("be", "dil", "cgh", "af"))
]
BLOCKS = [
    block for here, there in GROUPS for a, b in zip(here, there) for block in (a + (0,), b + (1,))
]
INDEX = {block: i for i, block in enumerate(BLOCKS)}
NBLOCK = len(BLOCKS)
SENDS = [
    BLOCKS,
    [
        block
        for here, there in GROUPS
        for a, b in zip(here, there)
        for block in (mirrored(b) + (1,), mirrored(a) + (0,))
    ],
]
GROUP = NBLOCK // 4
DETOURS = (NCH, 0)


def layer_kernel(
    routes_hbm, levels_hbm, frames_hbm, grads_hbm, wg_hbm, wu_hbm, wd_hbm,
    og_ref, ou_ref, od_ref, frame_ref,
    routes_ref, levels_ref, frames_ref, grads_ref,
    place_ref, gate_ref, pick_ref, scaled_ref, send_ref, recv, wts, turned, acts,
    sendp, recvp, passing, own_half, sib_send, sib_recv, ret, back, outs, outq, frame_out,
    i_sem, w_sem, loc_sem, d_send, d_recv, s_send, s_recv, p_send, p_recv, n_send, n_recv,
    h_send, h_recv, r_send, r_recv, rl_sem, q_send, q_recv, o_sem, f_sem,
):
    e = lax.axis_index("expert")
    c = lax.axis_index("etp")
    z = lax.axis_index("dp")
    ex, ey = e // 4, lax.rem(e, 4)
    odd = lax.rem(ex + ey, 2) == 1
    low, high = z + 1 - 2 * lax.rem(z, 2), 3 - z
    p, q = jnp.where(odd, high, low), jnp.where(odd, low, high)
    o = lax.rem(z + 2, 4)
    here, there = z // 2, lax.rem((z + 1) // 2, 2)
    own, own_flip = jnp.where(odd, there, here), jnp.where(odd, here, there)
    plane = (z, q)
    out_refs = (og_ref, ou_ref, od_ref)

    loads = [
        pltpu.make_async_copy(source, target, i_sem.at[i])
        for i, (source, target) in enumerate(
            (
                (routes_hbm, routes_ref),
                (levels_hbm, levels_ref),
                (frames_hbm, frames_ref),
                (grads_hbm, grads_ref),
            )
        )
    ]
    for load in loads:
        load.start()
    barrier = pltpu.get_barrier_semaphore()

    def at(dx, dy):
        return lax.rem(ex + dx, 4) * 4 + lax.rem(ey + dy, 4)

    def greet(i, _):
        d = lax.rem(e + i, PEERS)
        pl.semaphore_signal(barrier, inc=1, device_id=(d, c, q), device_id_type=MESH)

        @pl.when(i > 0)
        def _():
            pl.semaphore_signal(barrier, inc=1, device_id=(d, c, z), device_id_type=MESH)

        return 0

    lax.fori_loop(0, PEERS, greet, 0)
    for dx in range(4):
        for dy in range(4):
            if (dx + dy) % 2 == 1:
                pl.semaphore_signal(
                    barrier, inc=1, device_id=(at(dx, dy), c, p), device_id_type=MESH
                )
    pl.semaphore_signal(barrier, inc=1, device_id=(e, c, p), device_id_type=MESH)
    pl.semaphore_signal(barrier, inc=1, device_id=(e, 1 - c, z), device_id_type=MESH)

    wcopy = [
        pltpu.make_async_copy(w.at[own], wts.at[i], w_sem.at[i])
        for i, w in enumerate((wg_hbm, wu_hbm, wd_hbm))
    ]
    for w in wcopy:
        w.start()

    for load in loads:
        load.wait()

    ids = lax.broadcasted_iota(jnp.int32, (EXPERTS, TOK), 0)
    first = ids == routes_ref[0:1, :]
    second = ids == routes_ref[1:2, :]
    named = first | second
    before = lax.broadcasted_iota(jnp.int32, (TOK, TOK), 0) < lax.broadcasted_iota(
        jnp.int32, (TOK, TOK), 1
    )
    count = jnp.dot(
        named.astype(F32).astype(BF), before.astype(F32).astype(BF), preferred_element_type=F32
    )
    place_ref[...] = jnp.where(named, count, -1.0)
    level = jnp.where(first, levels_ref[0:1, :], levels_ref[1:2, :])
    gate_ref[...] = level.astype(F32) / 256.0
    slots = lax.broadcasted_iota(jnp.int32, (CAP, TOK), 0).astype(F32)

    def rows_of(i):
        return pl.ds(i * CAP if isinstance(i, int) else pl.multiple_of(i * CAP, CAP), CAP)

    def group_rows(g):
        return pl.ds(g * RB if isinstance(g, int) else pl.multiple_of(g * RB, RB), RB)

    def pack(g):
        for j in range(GROUP):
            dx, dy, k = BLOCKS[g * GROUP + j]
            theirs = own_flip if (dx + dy) % 2 else own
            expert = 2 * at(dx, dy) + (theirs if k == 0 else 1 - theirs)
            hit = place_ref[pl.ds(expert, 1), :] == slots
            pick_ref[rows_of(j), :] = jnp.where(hit, 1.0, 0.0).astype(BF)
            scaled_ref[rows_of(j), :] = jnp.where(hit, gate_ref[pl.ds(expert, 1), :], 0.0).astype(BF)
        rows = group_rows(g)
        send_ref[rows, 0:HALF] = jnp.dot(
            pick_ref[...], frames_ref[...], preferred_element_type=F32
        ).astype(BF)
        send_ref[rows, HALF : 2 * HALF] = jnp.dot(
            scaled_ref[...], grads_ref[...], preferred_element_type=F32
        ).astype(BF)

    def choose(a, b):
        return a if a == b else jnp.where(c == 0, a, b)

    def give(t):
        one, two = SENDS[0][t], SENDS[1][t]
        kinds = [k * (1 + (dx + dy) % 2) for dx, dy, k in (one, two)]
        dx, dy, _, i = [
            choose(a, b) for a, b in zip(one + (INDEX[one],), two + (INDEX[two],))
        ]
        kind = choose(*kinds)
        return pltpu.make_async_remote_copy(
            src_ref=send_ref.at[rows_of(i)],
            dst_ref=recv.at[c, rows_of(i)],
            send_sem=d_send.at[i],
            recv_sem=d_recv.at[i],
            device_id=(at(dx, dy), c, jnp.where(kind == 0, z, jnp.where(kind == 1, q, p))),
            device_id_type=MESH,
        )

    def take(i):
        return pltpu.make_async_remote_copy(
            src_ref=send_ref.at[rows_of(i)],
            dst_ref=recv.at[c, rows_of(i)],
            send_sem=d_send.at[i],
            recv_sem=d_recv.at[i],
            device_id=(e, c, q),
            device_id_type=MESH,
        )

    def share(half, i):
        return pltpu.make_async_remote_copy(
            src_ref=recv.at[half, rows_of(i)],
            dst_ref=recv.at[half, rows_of(i)],
            send_sem=s_send.at[i],
            recv_sem=s_recv.at[i],
            device_id=(e, 1 - c, z),
            device_id_type=MESH,
        )

    local = pltpu.make_async_copy(send_ref.at[rows_of(0)], recv.at[c, rows_of(0)], loc_sem)
    for g in range(4):
        pack(g)
        if g == 0:
            pl.semaphore_wait(barrier, 2 * PEERS + PEERS // 2 + 1)
            local.start()
        for t in range(g * GROUP, (g + 1) * GROUP):
            if SENDS[0][t] == (0, 0, 0):
                pl.when(c == 1)(lambda t=t: give(t).start())
            elif SENDS[1][t] == (0, 0, 0):
                pl.when(c == 0)(lambda t=t: give(t).start())
            else:
                give(t).start()
    for w in wcopy:
        w.wait()

    def arrive(g):
        for i in range(g * GROUP, (g + 1) * GROUP):
            if i == 0:
                local.wait()
            else:
                take(i).wait_recv()
            share(c, i).start()

        def mate(j, _):
            share(1 - c, g * GROUP + j).wait_recv()
            return 0

        lax.fori_loop(0, GROUP, mate, 0)

    def forward(g, ch):
        rows = group_rows(g)
        cols = pl.ds(pl.multiple_of(ch * CH, CH), CH)

        def product(i, base):
            total = jnp.dot(
                recv[0, rows, base : base + HALF], wts[i, 0:HALF, cols], preferred_element_type=F32
            )
            return total + jnp.dot(
                recv[1, rows, base : base + HALF], wts[i, HALF:D, cols], preferred_element_type=F32
            )

        pre_gate = product(0, 0)
        pre_up = product(1, 0)
        sig = jax.nn.sigmoid(pre_gate)
        act = pre_gate * sig
        acts[2, ch, rows, :] = (act * pre_up).astype(BF)
        grad = product(2, HALF)
        acts[0, ch, rows, :] = (
            grad * pre_up * sig * (1.0 + pre_gate * (1.0 - sig))
        ).astype(BF)
        acts[1, ch, rows, :] = (grad * act).astype(BF)

    def turn(g):
        rows = group_rows(g)

        def body(half, _):
            for t in range(2):
                for h in range(2):
                    base = t * HALF + h * SL
                    turned[t, 2 * half + h, :, rows] = recv[half, rows, base : base + SL].T
            return 0

        lax.fori_loop(0, 2, body, 0)

    def turn_part(g, part):
        rows = group_rows(g)
        for t in range(2):
            cols = pl.ds(pl.multiple_of(t * HALF + lax.rem(part, 2) * SL, SL), SL)
            turned[t, part, :, rows] = recv[part // 2, rows, cols].T

    def early(i, _):
        forward(i // NCH, lax.rem(i, NCH))
        return 0

    for g in range(4):
        arrive(g)
        if g < 3:
            turn(g)
            lax.fori_loop(g * NCH, (g + 1) * NCH, early, 0)

    def to_mate(ch, m, i):
        return pltpu.make_async_remote_copy(
            src_ref=sendp.at[i, ch, m],
            dst_ref=recvp.at[i, ch, m],
            send_sem=p_send.at[i, ch, m],
            recv_sem=p_recv.at[i, ch, m],
            device_id=(e, c, p),
            device_id_type=MESH,
        )

    def to_next(ch, i):
        return pltpu.make_async_remote_copy(
            src_ref=sendp.at[i, ch, 0],
            dst_ref=passing.at[i, ch],
            send_sem=p_send.at[i, ch, 0],
            recv_sem=n_recv.at[i, ch],
            device_id=(at(1, 0), c, p),
            device_id_type=MESH,
        )

    def from_next(ch, i):
        return pltpu.make_async_remote_copy(
            src_ref=passing.at[i, ch],
            dst_ref=recvp.at[i, ch, 0],
            send_sem=n_send.at[i, ch],
            recv_sem=p_recv.at[i, ch, 0],
            device_id=(at(3, 0), c, z),
            device_id_type=MESH,
        )

    def hand_on(i):
        def body(ch, _):
            to_next(ch, i).wait_recv()
            from_next(ch, i).start()
            return 0

        lax.fori_loop(0, DETOURS[i], body, 0)

    def dispatch_slice(ch, m, i):
        if m > 0 or DETOURS[i] == 0:
            to_mate(ch, m, i).start()
        elif DETOURS[i] == NCH:
            to_next(ch, i).start()
        else:
            pl.when(ch < DETOURS[i])(lambda: to_next(ch, i).start())
            pl.when(ch >= DETOURS[i])(lambda: to_mate(ch, m, i).start())

    def weight_grad(m, ch, part):
        lhs = turned[0 if m < 2 else 1, part]
        return jnp.dot(lhs, acts[m, ch], preferred_element_type=F32)

    def beyond(ch, _):
        def rest(g, _):
            forward(g, ch)
            return 0

        lax.fori_loop(3, 4, rest, 0)
        for m in (1, 0, 2):
            sendp[0, ch, m] = weight_grad(m, ch, o).astype(BF)
            dispatch_slice(ch, m, 0)
        return 0

    turn_part(3, o)
    lax.fori_loop(0, NCH, beyond, 0)
    for part in (p, q, z):
        turn_part(3, part)

    def swap(b):
        return pltpu.make_async_remote_copy(
            src_ref=sib_send.at[b],
            dst_ref=sib_recv.at[b],
            send_sem=h_send.at[b],
            recv_sem=h_recv.at[b],
            device_id=(e, 1 - c, z),
            device_id_type=MESH,
        )

    def input_grad(b, _):
        rows = group_rows(b)

        def half_of(h):
            feats = pl.ds(pl.multiple_of(h * HALF, HALF), HALF)
            total = jnp.zeros((RB, HALF), F32)
            for w in range(2):
                for ch in range(NCH):
                    total += lax.dot_general(
                        acts[w, ch, rows, :],
                        wts[w, feats, ch * CH : (ch + 1) * CH],
                        (((1,), (1,)), ((), ())),
                        preferred_element_type=F32,
                    )
            return total

        sib_send[b] = half_of(1 - c).astype(BF)
        swap(b).start()
        own_half[b] = half_of(c)
        return 0

    lax.fori_loop(0, 4, input_grad, 0)
    hand_on(0)

    def ending(ch, _):
        for m in range(3):
            sendp[1, ch, m] = weight_grad(m, ch, p).astype(BF)
            dispatch_slice(ch, m, 1)
        return 0


    def give_back(i):
        dx, dy, k = BLOCKS[i]
        return pltpu.make_async_remote_copy(
            src_ref=ret.at[rows_of(i)],
            dst_ref=back.at[e, own],
            send_sem=r_send.at[i],
            recv_sem=r_recv.at[k, e],
            device_id=(at((4 - dx) % 4, (4 - dy) % 4), c, plane[k]),
            device_id_type=MESH,
        )

    def take_back(s, k):
        alike = lax.rem(s // 4 + lax.rem(s, 4), 2) == lax.rem(ex + ey, 2)
        theirs = jnp.where(alike, own, own_flip)
        return pltpu.make_async_remote_copy(
            src_ref=ret.at[rows_of(0)],
            dst_ref=back.at[s, theirs if k == 0 else 1 - theirs],
            send_sem=r_send.at[0],
            recv_sem=r_recv.at[k, s],
            device_id=(s, c, plane[k]),
            device_id_type=MESH,
        )

    back_local = pltpu.make_async_copy(ret.at[rows_of(0)], back.at[e, own], rl_sem)
    for b in range(4):
        swap(b).wait_recv()
        ret[group_rows(b), :] = (own_half[b] + sib_recv[b].astype(F32)).astype(BF)
        for i in range(b * GROUP, (b + 1) * GROUP):
            if i == 0:
                back_local.start()
            else:
                give_back(i).start()

    lax.fori_loop(0, NCH, ending, 0)

    def place_of(ch, m, expert):
        return out_refs[m].at[expert, :, pl.ds(pl.multiple_of(ch * CH, CH), CH)]

    def with_q(ch, m, expert):
        return pltpu.make_async_remote_copy(
            src_ref=outq.at[ch, m],
            dst_ref=place_of(ch, m, expert),
            send_sem=q_send.at[ch, m],
            recv_sem=q_recv.at[ch, m],
            device_id=(e, c, q),
            device_id_type=MESH,
        )

    def to_out(ch, m):
        return pltpu.make_async_copy(outs.at[ch, m], place_of(ch, m, own), o_sem.at[ch, m])

    def pass_on(ch, _):
        for m in (1, 2, 0):
            total = weight_grad(m, ch, q)
            to_mate(ch, m, 0).wait_recv()
            outq[ch, m] = (total + recvp[0, ch, m].astype(F32)).astype(BF)
            with_q(ch, m, own).start()
        return 0

    lax.fori_loop(0, NCH, pass_on, 0)
    hand_on(1)

    def finish(ch, _):
        for m in range(3):
            total = weight_grad(m, ch, z)
            to_mate(ch, m, 1).wait_recv()
            outs[ch, m] = (total + recvp[1, ch, m].astype(F32)).astype(BF)
            to_out(ch, m).start()
        return 0

    lax.fori_loop(0, NCH // 2, finish, 0)

    def drain_back(i, _):
        take_back(i, 1).wait_recv()

        @pl.when(i != e)
        def _():
            take_back(i, 0).wait_recv()

        return 0

    lax.fori_loop(0, PEERS, drain_back, 0)
    back_local.wait()
    total = jnp.zeros((TOK, HALF), F32)
    step = 8
    for g in range(EXPERTS // step):
        parts = []
        for j in range(step):
            x = g * step + j
            parts.append(jnp.where(place_ref[x : x + 1, :] == slots, 1.0, 0.0).astype(BF))
        pick = jnp.concatenate(parts, axis=0)
        rows = back[g * step // 2 : (g + 1) * step // 2].reshape(step * CAP, HALF)
        total += jnp.dot(pick.T, rows, preferred_element_type=F32)
    frame_out[...] = total.astype(BF)
    frame_copy = pltpu.make_async_copy(frame_out, frame_ref, f_sem)
    frame_copy.start()

    lax.fori_loop(NCH // 2, NCH, finish, 0)

    def drain_blocks(i, _):
        share(c, i).wait_send()

        @pl.when(i > 0)
        def _():
            take(i).wait_send()
            pltpu.make_async_remote_copy(
                src_ref=ret.at[rows_of(i)],
                dst_ref=back.at[e, own],
                send_sem=r_send.at[i],
                recv_sem=r_recv.at[0, e],
                device_id=(e, c, q),
                device_id_type=MESH,
            ).wait_send()

        return 0

    lax.fori_loop(0, NBLOCK, drain_blocks, 0)
    frame_copy.wait()

    def drain(ch, _):
        swap(ch).wait_send()
        for m in range(3):
            for i in range(2):
                to_mate(ch, m, i).wait_send()
            with_q(ch, m, own).wait_send()
            with_q(ch, m, 1 - own).wait_recv()
            to_out(ch, m).wait()
        return 0

    lax.fori_loop(0, NCH, drain, 0)

    for i in range(2):

        def drain_passing(ch, _, i=i):
            from_next(ch, i).wait_send()
            return 0

        lax.fori_loop(0, DETOURS[i], drain_passing, 0)


def layer(routes, levels, frames, out_grad, w_gate, w_up, w_down):
    dma = pltpu.SemaphoreType.DMA
    grad = jax.ShapeDtypeStruct((2, SL, FF), BF)
    return pl.pallas_call(
        layer_kernel,
        out_shape=[grad, grad, grad, jax.ShapeDtypeStruct((TOK, HALF), BF)],
        in_specs=[ANY] * 7,
        out_specs=[ANY] * 4,
        scratch_shapes=[
            pltpu.VMEM((2, TOK), jnp.int32),
            pltpu.VMEM((2, TOK), jnp.int32),
            pltpu.VMEM((TOK, HALF), BF),
            pltpu.VMEM((TOK, HALF), BF),
            pltpu.VMEM((EXPERTS, TOK), F32),
            pltpu.VMEM((EXPERTS, TOK), F32),
            pltpu.VMEM((RB, TOK), BF),
            pltpu.VMEM((RB, TOK), BF),
            pltpu.VMEM((ROWS, 2 * HALF), BF),
            pltpu.VMEM((2, ROWS, 2 * HALF), BF),
            pltpu.VMEM((3, D, FF), BF),
            pltpu.VMEM((2, DP, SL, ROWS), BF),
            pltpu.VMEM((3, NCH, ROWS, CH), BF),
            pltpu.VMEM((2, NCH, 3, SL, CH), BF),
            pltpu.VMEM((2, NCH, 3, SL, CH), BF),
            pltpu.VMEM((2, NCH, SL, CH), BF),
            pltpu.VMEM((4, RB, HALF), F32),
            pltpu.VMEM((4, RB, HALF), BF),
            pltpu.VMEM((4, RB, HALF), BF),
            pltpu.VMEM((ROWS, HALF), BF),
            pltpu.VMEM((PEERS, 2, CAP, HALF), BF),
            pltpu.VMEM((NCH, 3, SL, CH), BF),
            pltpu.VMEM((NCH, 3, SL, CH), BF),
            pltpu.VMEM((TOK, HALF), BF),
            dma((4,)),
            dma((3,)),
            dma,
            dma((NBLOCK,)),
            dma((NBLOCK,)),
            dma((NBLOCK,)),
            dma((NBLOCK,)),
            dma((2, NCH, 3)),
            dma((2, NCH, 3)),
            dma((2, NCH)),
            dma((2, NCH)),
            dma((4,)),
            dma((4,)),
            dma((NBLOCK,)),
            dma((2, PEERS)),
            dma,
            dma((NCH, 3)),
            dma((NCH, 3)),
            dma((NCH, 3)),
            dma,
        ],
        compiler_params=pltpu.CompilerParams(
            collective_id=1, has_side_effects=True, vmem_limit_bytes=60 * 1024 * 1024
        ),
        cost_estimate=pl.CostEstimate(
            flops=16 * ROWS * D * FF, bytes_accessed=20_000_000, transcendentals=ROWS * FF
        ),
        name="layer",
    )(routes, levels, frames, out_grad, w_gate, w_up, w_down)


def settle_kernel(*refs):
    n = (len(refs) - 2) // 3
    ins, outs, held = refs[:n], refs[n : 2 * n], refs[2 * n : 3 * n]
    in_sem, out_sem = refs[3 * n :]
    pieces = []
    for i in range(n):
        rows = ins[i].shape[-2] // (4 if ins[i].ndim == 2 else 2)
        for j in range(4):
            part = pl.ds(j * rows, rows) if ins[i].ndim == 2 else (j // 2, pl.ds(j % 2 * rows, rows))
            pieces.append(
                (
                    pltpu.make_async_copy(ins[i].at[part], held[i].at[part], in_sem.at[i, j]),
                    pltpu.make_async_copy(held[i].at[part], outs[i].at[part], out_sem.at[i, j]),
                )
            )
    for load, _ in pieces:
        load.start()
    for load, store in pieces:
        load.wait()
        store.start()
    for _, store in pieces:
        store.wait()


def settle(*arrays):
    n = len(arrays)
    return pl.pallas_call(
        settle_kernel,
        out_shape=[jax.ShapeDtypeStruct(a.shape, a.dtype) for a in arrays],
        in_specs=[ANY] * n,
        out_specs=[ANY] * n,
        scratch_shapes=[pltpu.VMEM(a.shape, a.dtype) for a in arrays]
        + [pltpu.SemaphoreType.DMA((n, 4))] * 2,
        name="settle",
    )(*arrays)


def local(frames, out_grad, routes, gate_levels, w_gate, w_up, w_down):
    gate_grad, up_grad, down_grad, frame_grad = settle(
        *layer(routes.T, gate_levels.T, frames, out_grad, w_gate, w_up, w_down)
    )
    return frame_grad, gate_grad, up_grad, down_grad


def solution(mesh):
    placed = (
        P(("expert", "dp"), "etp"),
        P(("expert", "dp"), "etp"),
        P(("expert", "dp"), None),
        P(("expert", "dp"), None),
        P("expert", None, "etp"),
        P("expert", None, "etp"),
        P("expert", None, "etp"),
    )
    return jax.shard_map(
        local,
        mesh=mesh,
        in_specs=placed,
        out_specs=(
            P(("expert", "dp"), "etp"),
            P("expert", "dp", "etp"),
            P("expert", "dp", "etp"),
            P("expert", "dp", "etp"),
        ),
        check_vma=False,
    )
```

```python
import jax
import jax.numpy as jnp
from jax import lax
from jax.experimental import pallas as pl
from jax.experimental.pallas import tpu as pltpu
from jax.sharding import PartitionSpec as P

MESH = pl.DeviceIdType.MESH
BF, F32 = jnp.bfloat16, jnp.float32
PEERS, DP = 16, 4
EXPERTS = 32
CAP = 48
TOK = 384
D = 1024
HALF = 512
FF = 1024
ROWS = 2 * PEERS * CAP
CH = 256
NCH = FF // CH
SL = D // DP
RB = 384
ANY = pl.BlockSpec(memory_space=pl.ANY)


def offsets(names):
    kinds = {
        "a": [(1, 0), (3, 0)], "b": [(0, 1), (0, 3)], "c": [(1, 1), (3, 3)], "d": [(1, 3), (3, 1)],
        "e": [(2, 1), (2, 3)], "f": [(1, 2), (3, 2)], "g": [(2, 0)], "h": [(0, 2)], "i": [(2, 2)],
        "l": [(0, 0)],
    }
    return [off for name in names for off in kinds[name]]


def mirrored(off):
    return (4 - off[0]) % 4, (4 - off[1]) % 4


GROUPS = [
    (offsets(here), offsets(there))
    for here, there in zip(("lid", "af", "be", "cgh"), ("be", "dil", "cgh", "af"))
]
BLOCKS = [
    block for here, there in GROUPS for a, b in zip(here, there) for block in (a + (0,), b + (1,))
]
INDEX = {block: i for i, block in enumerate(BLOCKS)}
NBLOCK = len(BLOCKS)
SENDS = [
    BLOCKS,
    [
        block
        for here, there in GROUPS
        for a, b in zip(here, there)
        for block in (mirrored(b) + (1,), mirrored(a) + (0,))
    ],
]
GROUP = NBLOCK // 4
DETOURS = (NCH, 0)


def layer_kernel(
    routes_hbm, levels_hbm, frames_hbm, grads_hbm, wg_hbm, wu_hbm, wd_hbm,
    og_ref, ou_ref, od_ref, frame_ref,
    routes_ref, levels_ref, frames_ref, grads_ref,
    place_ref, gate_ref, pick_ref, scaled_ref, send_ref, recv, wts, turned, acts,
    sendp, recvp, passing, own_half, sib_send, sib_recv, ret, back, outs, outq, frame_out,
    i_sem, w_sem, loc_sem, d_send, d_recv, s_send, s_recv, p_send, p_recv, n_send, n_recv,
    h_send, h_recv, r_send, r_recv, rl_sem, q_send, q_recv, o_sem, f_sem,
):
    e = lax.axis_index("expert")
    c = lax.axis_index("etp")
    z = lax.axis_index("dp")
    ex, ey = e // 4, lax.rem(e, 4)
    odd = lax.rem(ex + ey, 2) == 1
    low, high = z + 1 - 2 * lax.rem(z, 2), 3 - z
    p, q = jnp.where(odd, high, low), jnp.where(odd, low, high)
    o = lax.rem(z + 2, 4)
    here, there = z // 2, lax.rem((z + 1) // 2, 2)
    own, own_flip = jnp.where(odd, there, here), jnp.where(odd, here, there)
    plane = (z, q)
    out_refs = (og_ref, ou_ref, od_ref)

    loads = [
        pltpu.make_async_copy(source, target, i_sem.at[i])
        for i, (source, target) in enumerate(
            (
                (routes_hbm, routes_ref),
                (levels_hbm, levels_ref),
                (frames_hbm, frames_ref),
                (grads_hbm, grads_ref),
            )
        )
    ]
    for load in loads:
        load.start()
    barrier = pltpu.get_barrier_semaphore()

    def at(dx, dy):
        return lax.rem(ex + dx, 4) * 4 + lax.rem(ey + dy, 4)

    def greet(i, _):
        d = lax.rem(e + i, PEERS)
        pl.semaphore_signal(barrier, inc=1, device_id=(d, c, q), device_id_type=MESH)

        @pl.when(i > 0)
        def _():
            pl.semaphore_signal(barrier, inc=1, device_id=(d, c, z), device_id_type=MESH)

        return 0

    lax.fori_loop(0, PEERS, greet, 0)
    for dx in range(4):
        for dy in range(4):
            if (dx + dy) % 2 == 1:
                pl.semaphore_signal(
                    barrier, inc=1, device_id=(at(dx, dy), c, p), device_id_type=MESH
                )
    pl.semaphore_signal(barrier, inc=1, device_id=(e, c, p), device_id_type=MESH)
    pl.semaphore_signal(barrier, inc=1, device_id=(e, 1 - c, z), device_id_type=MESH)

    wcopy = [
        pltpu.make_async_copy(w.at[own], wts.at[i], w_sem.at[i])
        for i, w in enumerate((wg_hbm, wu_hbm, wd_hbm))
    ]
    for w in wcopy:
        w.start()

    for load in loads:
        load.wait()

    ids = lax.broadcasted_iota(jnp.int32, (EXPERTS, TOK), 0)
    first = ids == routes_ref[0:1, :]
    second = ids == routes_ref[1:2, :]
    named = first | second
    before = lax.broadcasted_iota(jnp.int32, (TOK, TOK), 0) < lax.broadcasted_iota(
        jnp.int32, (TOK, TOK), 1
    )
    count = jnp.dot(
        named.astype(F32).astype(BF), before.astype(F32).astype(BF), preferred_element_type=F32
    )
    place_ref[...] = jnp.where(named, count, -1.0)
    level = jnp.where(first, levels_ref[0:1, :], levels_ref[1:2, :])
    gate_ref[...] = level.astype(F32) / 256.0
    slots = lax.broadcasted_iota(jnp.int32, (CAP, TOK), 0).astype(F32)

    def rows_of(i):
        return pl.ds(i * CAP if isinstance(i, int) else pl.multiple_of(i * CAP, CAP), CAP)

    def group_rows(g):
        return pl.ds(g * RB if isinstance(g, int) else pl.multiple_of(g * RB, RB), RB)

    def pack(g):
        for j in range(GROUP):
            dx, dy, k = BLOCKS[g * GROUP + j]
            theirs = own_flip if (dx + dy) % 2 else own
            expert = 2 * at(dx, dy) + (theirs if k == 0 else 1 - theirs)
            hit = place_ref[pl.ds(expert, 1), :] == slots
            pick_ref[rows_of(j), :] = jnp.where(hit, 1.0, 0.0).astype(BF)
            scaled_ref[rows_of(j), :] = jnp.where(hit, gate_ref[pl.ds(expert, 1), :], 0.0).astype(BF)
        rows = group_rows(g)
        send_ref[rows, 0:HALF] = jnp.dot(
            pick_ref[...], frames_ref[...], preferred_element_type=F32
        ).astype(BF)
        send_ref[rows, HALF : 2 * HALF] = jnp.dot(
            scaled_ref[...], grads_ref[...], preferred_element_type=F32
        ).astype(BF)

    def choose(a, b):
        return a if a == b else jnp.where(c == 0, a, b)

    def give(t):
        one, two = SENDS[0][t], SENDS[1][t]
        kinds = [k * (1 + (dx + dy) % 2) for dx, dy, k in (one, two)]
        dx, dy, _, i = [
            choose(a, b) for a, b in zip(one + (INDEX[one],), two + (INDEX[two],))
        ]
        kind = choose(*kinds)
        return pltpu.make_async_remote_copy(
            src_ref=send_ref.at[rows_of(i)],
            dst_ref=recv.at[c, rows_of(i)],
            send_sem=d_send.at[i],
            recv_sem=d_recv.at[i],
            device_id=(at(dx, dy), c, jnp.where(kind == 0, z, jnp.where(kind == 1, q, p))),
            device_id_type=MESH,
        )

    def take(i):
        return pltpu.make_async_remote_copy(
            src_ref=send_ref.at[rows_of(i)],
            dst_ref=recv.at[c, rows_of(i)],
            send_sem=d_send.at[i],
            recv_sem=d_recv.at[i],
            device_id=(e, c, q),
            device_id_type=MESH,
        )

    def share(half, i):
        return pltpu.make_async_remote_copy(
            src_ref=recv.at[half, rows_of(i)],
            dst_ref=recv.at[half, rows_of(i)],
            send_sem=s_send.at[i],
            recv_sem=s_recv.at[i],
            device_id=(e, 1 - c, z),
            device_id_type=MESH,
        )

    local = pltpu.make_async_copy(send_ref.at[rows_of(0)], recv.at[c, rows_of(0)], loc_sem)
    for g in range(4):
        pack(g)
        if g == 0:
            pl.semaphore_wait(barrier, 2 * PEERS + PEERS // 2 + 1)
            local.start()
        for t in range(g * GROUP, (g + 1) * GROUP):
            if SENDS[0][t] == (0, 0, 0):
                pl.when(c == 1)(lambda t=t: give(t).start())
            elif SENDS[1][t] == (0, 0, 0):
                pl.when(c == 0)(lambda t=t: give(t).start())
            else:
                give(t).start()
    for w in wcopy:
        w.wait()

    def arrive(g):
        for i in range(g * GROUP, (g + 1) * GROUP):
            if i == 0:
                local.wait()
            else:
                take(i).wait_recv()
            share(c, i).start()

        def mate(j, _):
            share(1 - c, g * GROUP + j).wait_recv()
            return 0

        lax.fori_loop(0, GROUP, mate, 0)

    def forward(g, ch):
        rows = group_rows(g)
        cols = pl.ds(pl.multiple_of(ch * CH, CH), CH)

        def product(i, base):
            total = jnp.dot(
                recv[0, rows, base : base + HALF], wts[i, 0:HALF, cols], preferred_element_type=F32
            )
            return total + jnp.dot(
                recv[1, rows, base : base + HALF], wts[i, HALF:D, cols], preferred_element_type=F32
            )

        pre_gate = product(0, 0)
        pre_up = product(1, 0)
        sig = jax.nn.sigmoid(pre_gate)
        act = pre_gate * sig
        acts[2, ch, rows, :] = (act * pre_up).astype(BF)
        grad = product(2, HALF)
        acts[0, ch, rows, :] = (
            grad * pre_up * sig * (1.0 + pre_gate * (1.0 - sig))
        ).astype(BF)
        acts[1, ch, rows, :] = (grad * act).astype(BF)

    def turn(g):
        rows = group_rows(g)

        def body(half, _):
            for t in range(2):
                for h in range(2):
                    base = t * HALF + h * SL
                    turned[t, 2 * half + h, :, rows] = recv[half, rows, base : base + SL].T
            return 0

        lax.fori_loop(0, 2, body, 0)

    def turn_part(g, part):
        rows = group_rows(g)
        for t in range(2):
            cols = pl.ds(pl.multiple_of(t * HALF + lax.rem(part, 2) * SL, SL), SL)
            turned[t, part, :, rows] = recv[part // 2, rows, cols].T

    def early(i, _):
        forward(i // NCH, lax.rem(i, NCH))
        return 0

    for g in range(4):
        arrive(g)
        if g < 3:
            turn(g)
            lax.fori_loop(g * NCH, (g + 1) * NCH, early, 0)

    def to_mate(ch, m, i):
        return pltpu.make_async_remote_copy(
            src_ref=sendp.at[i, ch, m],
            dst_ref=recvp.at[i, ch, m],
            send_sem=p_send.at[i, ch, m],
            recv_sem=p_recv.at[i, ch, m],
            device_id=(e, c, p),
            device_id_type=MESH,
        )

    def to_next(ch, i):
        return pltpu.make_async_remote_copy(
            src_ref=sendp.at[i, ch, 0],
            dst_ref=passing.at[i, ch],
            send_sem=p_send.at[i, ch, 0],
            recv_sem=n_recv.at[i, ch],
            device_id=(at(1, 0), c, p),
            device_id_type=MESH,
        )

    def from_next(ch, i):
        return pltpu.make_async_remote_copy(
            src_ref=passing.at[i, ch],
            dst_ref=recvp.at[i, ch, 0],
            send_sem=n_send.at[i, ch],
            recv_sem=p_recv.at[i, ch, 0],
            device_id=(at(3, 0), c, z),
            device_id_type=MESH,
        )

    def hand_on(i):
        def body(ch, _):
            to_next(ch, i).wait_recv()
            from_next(ch, i).start()
            return 0

        lax.fori_loop(0, DETOURS[i], body, 0)

    def dispatch_slice(ch, m, i):
        if m > 0 or DETOURS[i] == 0:
            to_mate(ch, m, i).start()
        elif DETOURS[i] == NCH:
            to_next(ch, i).start()
        else:
            pl.when(ch < DETOURS[i])(lambda: to_next(ch, i).start())
            pl.when(ch >= DETOURS[i])(lambda: to_mate(ch, m, i).start())

    def weight_grad(m, ch, part):
        lhs = turned[0 if m < 2 else 1, part]
        return jnp.dot(lhs, acts[m, ch], preferred_element_type=F32)

    def beyond(ch, _):
        def rest(g, _):
            forward(g, ch)
            return 0

        lax.fori_loop(3, 4, rest, 0)
        for m in (1, 2, 0):
            sendp[0, ch, m] = weight_grad(m, ch, o).astype(BF)
            dispatch_slice(ch, m, 0)
        return 0

    turn_part(3, o)
    lax.fori_loop(0, NCH, beyond, 0)
    for part in (p, q, z):
        turn_part(3, part)

    def swap(b):
        return pltpu.make_async_remote_copy(
            src_ref=sib_send.at[b],
            dst_ref=sib_recv.at[b],
            send_sem=h_send.at[b],
            recv_sem=h_recv.at[b],
            device_id=(e, 1 - c, z),
            device_id_type=MESH,
        )

    def input_grad(b, _):
        rows = group_rows(b)

        def half_of(h):
            feats = pl.ds(pl.multiple_of(h * HALF, HALF), HALF)
            total = jnp.zeros((RB, HALF), F32)
            for w in range(2):
                for ch in range(NCH):
                    total += lax.dot_general(
                        acts[w, ch, rows, :],
                        wts[w, feats, ch * CH : (ch + 1) * CH],
                        (((1,), (1,)), ((), ())),
                        preferred_element_type=F32,
                    )
            return total

        sib_send[b] = half_of(1 - c).astype(BF)
        swap(b).start()
        own_half[b] = half_of(c)
        return 0

    lax.fori_loop(0, 4, input_grad, 0)
    hand_on(0)

    def ending(ch, _):
        for m in range(3):
            sendp[1, ch, m] = weight_grad(m, ch, p).astype(BF)
            dispatch_slice(ch, m, 1)
        return 0


    def give_back(i):
        dx, dy, k = BLOCKS[i]
        return pltpu.make_async_remote_copy(
            src_ref=ret.at[rows_of(i)],
            dst_ref=back.at[e, own],
            send_sem=r_send.at[i],
            recv_sem=r_recv.at[k, e],
            device_id=(at((4 - dx) % 4, (4 - dy) % 4), c, plane[k]),
            device_id_type=MESH,
        )

    def take_back(s, k):
        alike = lax.rem(s // 4 + lax.rem(s, 4), 2) == lax.rem(ex + ey, 2)
        theirs = jnp.where(alike, own, own_flip)
        return pltpu.make_async_remote_copy(
            src_ref=ret.at[rows_of(0)],
            dst_ref=back.at[s, theirs if k == 0 else 1 - theirs],
            send_sem=r_send.at[0],
            recv_sem=r_recv.at[k, s],
            device_id=(s, c, plane[k]),
            device_id_type=MESH,
        )

    back_local = pltpu.make_async_copy(ret.at[rows_of(0)], back.at[e, own], rl_sem)
    for b in range(4):
        swap(b).wait_recv()
        ret[group_rows(b), :] = (own_half[b] + sib_recv[b].astype(F32)).astype(BF)
        for i in range(b * GROUP, (b + 1) * GROUP):
            if i == 0:
                back_local.start()
            else:
                give_back(i).start()

    lax.fori_loop(0, NCH, ending, 0)

    def place_of(ch, m, expert):
        return out_refs[m].at[expert, :, pl.ds(pl.multiple_of(ch * CH, CH), CH)]

    def with_q(ch, m, expert):
        return pltpu.make_async_remote_copy(
            src_ref=outq.at[ch, m],
            dst_ref=place_of(ch, m, expert),
            send_sem=q_send.at[ch, m],
            recv_sem=q_recv.at[ch, m],
            device_id=(e, c, q),
            device_id_type=MESH,
        )

    def to_out(ch, m):
        return pltpu.make_async_copy(outs.at[ch, m], place_of(ch, m, own), o_sem.at[ch, m])

    def pass_on(ch, _):
        for m in (1, 2, 0):
            total = weight_grad(m, ch, q)
            to_mate(ch, m, 0).wait_recv()
            outq[ch, m] = (total + recvp[0, ch, m].astype(F32)).astype(BF)
            with_q(ch, m, own).start()
        return 0

    lax.fori_loop(0, NCH, pass_on, 0)
    hand_on(1)

    def finish(ch, _):
        for m in range(3):
            total = weight_grad(m, ch, z)
            to_mate(ch, m, 1).wait_recv()
            outs[ch, m] = (total + recvp[1, ch, m].astype(F32)).astype(BF)
            to_out(ch, m).start()
        return 0

    lax.fori_loop(0, NCH // 2, finish, 0)

    def drain_back(i, _):
        take_back(i, 1).wait_recv()

        @pl.when(i != e)
        def _():
            take_back(i, 0).wait_recv()

        return 0

    lax.fori_loop(0, PEERS, drain_back, 0)
    back_local.wait()
    total = jnp.zeros((TOK, HALF), F32)
    step = 8
    for g in range(EXPERTS // step):
        parts = []
        for j in range(step):
            x = g * step + j
            parts.append(jnp.where(place_ref[x : x + 1, :] == slots, 1.0, 0.0).astype(BF))
        pick = jnp.concatenate(parts, axis=0)
        rows = back[g * step // 2 : (g + 1) * step // 2].reshape(step * CAP, HALF)
        total += jnp.dot(pick.T, rows, preferred_element_type=F32)
    frame_out[...] = total.astype(BF)
    frame_copy = pltpu.make_async_copy(frame_out, frame_ref, f_sem)
    frame_copy.start()

    lax.fori_loop(NCH // 2, NCH, finish, 0)

    def drain_blocks(i, _):
        share(c, i).wait_send()

        @pl.when(i > 0)
        def _():
            take(i).wait_send()
            pltpu.make_async_remote_copy(
                src_ref=ret.at[rows_of(i)],
                dst_ref=back.at[e, own],
                send_sem=r_send.at[i],
                recv_sem=r_recv.at[0, e],
                device_id=(e, c, q),
                device_id_type=MESH,
            ).wait_send()

        return 0

    lax.fori_loop(0, NBLOCK, drain_blocks, 0)
    frame_copy.wait()

    def drain(ch, _):
        swap(ch).wait_send()
        for m in range(3):
            for i in range(2):
                to_mate(ch, m, i).wait_send()
            with_q(ch, m, own).wait_send()
            with_q(ch, m, 1 - own).wait_recv()
            to_out(ch, m).wait()
        return 0

    lax.fori_loop(0, NCH, drain, 0)

    for i in range(2):

        def drain_passing(ch, _, i=i):
            from_next(ch, i).wait_send()
            return 0

        lax.fori_loop(0, DETOURS[i], drain_passing, 0)


def layer(routes, levels, frames, out_grad, w_gate, w_up, w_down):
    dma = pltpu.SemaphoreType.DMA
    grad = jax.ShapeDtypeStruct((2, SL, FF), BF)
    return pl.pallas_call(
        layer_kernel,
        out_shape=[grad, grad, grad, jax.ShapeDtypeStruct((TOK, HALF), BF)],
        in_specs=[ANY] * 7,
        out_specs=[ANY] * 4,
        scratch_shapes=[
            pltpu.VMEM((2, TOK), jnp.int32),
            pltpu.VMEM((2, TOK), jnp.int32),
            pltpu.VMEM((TOK, HALF), BF),
            pltpu.VMEM((TOK, HALF), BF),
            pltpu.VMEM((EXPERTS, TOK), F32),
            pltpu.VMEM((EXPERTS, TOK), F32),
            pltpu.VMEM((RB, TOK), BF),
            pltpu.VMEM((RB, TOK), BF),
            pltpu.VMEM((ROWS, 2 * HALF), BF),
            pltpu.VMEM((2, ROWS, 2 * HALF), BF),
            pltpu.VMEM((3, D, FF), BF),
            pltpu.VMEM((2, DP, SL, ROWS), BF),
            pltpu.VMEM((3, NCH, ROWS, CH), BF),
            pltpu.VMEM((2, NCH, 3, SL, CH), BF),
            pltpu.VMEM((2, NCH, 3, SL, CH), BF),
            pltpu.VMEM((2, NCH, SL, CH), BF),
            pltpu.VMEM((4, RB, HALF), F32),
            pltpu.VMEM((4, RB, HALF), BF),
            pltpu.VMEM((4, RB, HALF), BF),
            pltpu.VMEM((ROWS, HALF), BF),
            pltpu.VMEM((PEERS, 2, CAP, HALF), BF),
            pltpu.VMEM((NCH, 3, SL, CH), BF),
            pltpu.VMEM((NCH, 3, SL, CH), BF),
            pltpu.VMEM((TOK, HALF), BF),
            dma((4,)),
            dma((3,)),
            dma,
            dma((NBLOCK,)),
            dma((NBLOCK,)),
            dma((NBLOCK,)),
            dma((NBLOCK,)),
            dma((2, NCH, 3)),
            dma((2, NCH, 3)),
            dma((2, NCH)),
            dma((2, NCH)),
            dma((4,)),
            dma((4,)),
            dma((NBLOCK,)),
            dma((2, PEERS)),
            dma,
            dma((NCH, 3)),
            dma((NCH, 3)),
            dma((NCH, 3)),
            dma,
        ],
        compiler_params=pltpu.CompilerParams(
            collective_id=1, has_side_effects=True, vmem_limit_bytes=60 * 1024 * 1024
        ),
        cost_estimate=pl.CostEstimate(
            flops=16 * ROWS * D * FF, bytes_accessed=20_000_000, transcendentals=ROWS * FF
        ),
        name="layer",
    )(routes, levels, frames, out_grad, w_gate, w_up, w_down)


def settle_kernel(*refs):
    n = (len(refs) - 2) // 3
    ins, outs, held = refs[:n], refs[n : 2 * n], refs[2 * n : 3 * n]
    in_sem, out_sem = refs[3 * n :]
    pieces = []
    for i in range(n):
        rows = ins[i].shape[-2] // (4 if ins[i].ndim == 2 else 2)
        for j in range(4):
            part = pl.ds(j * rows, rows) if ins[i].ndim == 2 else (j // 2, pl.ds(j % 2 * rows, rows))
            pieces.append(
                (
                    pltpu.make_async_copy(ins[i].at[part], held[i].at[part], in_sem.at[i, j]),
                    pltpu.make_async_copy(held[i].at[part], outs[i].at[part], out_sem.at[i, j]),
                )
            )
    for load, _ in pieces:
        load.start()
    for load, store in pieces:
        load.wait()
        store.start()
    for _, store in pieces:
        store.wait()


def settle(*arrays):
    n = len(arrays)
    return pl.pallas_call(
        settle_kernel,
        out_shape=[jax.ShapeDtypeStruct(a.shape, a.dtype) for a in arrays],
        in_specs=[ANY] * n,
        out_specs=[ANY] * n,
        scratch_shapes=[pltpu.VMEM(a.shape, a.dtype) for a in arrays]
        + [pltpu.SemaphoreType.DMA((n, 4))] * 2,
        name="settle",
    )(*arrays)


def local(frames, out_grad, routes, gate_levels, w_gate, w_up, w_down):
    gate_grad, up_grad, down_grad, frame_grad = settle(
        *layer(routes.T, gate_levels.T, frames, out_grad, w_gate, w_up, w_down)
    )
    return frame_grad, gate_grad, up_grad, down_grad


def solution(mesh):
    placed = (
        P(("expert", "dp"), "etp"),
        P(("expert", "dp"), "etp"),
        P(("expert", "dp"), None),
        P(("expert", "dp"), None),
        P("expert", None, "etp"),
        P("expert", None, "etp"),
        P("expert", None, "etp"),
    )
    return jax.shard_map(
        local,
        mesh=mesh,
        in_specs=placed,
        out_specs=(
            P(("expert", "dp"), "etp"),
            P("expert", "dp", "etp"),
            P("expert", "dp", "etp"),
            P("expert", "dp", "etp"),
        ),
        check_vma=False,
    )
```
